512 devices in a mesh: role: 2 (over core), grp: 64 (over y, z), tp: 4 (over x).
Axes of the slice: x: 4, y: 8, z: 8, core: 2. Of those that a mesh axis runs over, the one named last changes fastest.
Arguments:
- q_latent: bfloat16 [256, 128, 576], P(('role', 'grp')), may hold values from -6 to 6
- key_value_cache: bfloat16 [256, 1024, 576], P(('role', 'grp'), 'tp'), may hold values from -6 to 6
- cache_lengths: int32 [256], P(('role', 'grp')), may hold values from 2 to 1024, as said below
- hidden: bfloat16 [8192, 7168], P('grp', ('role', 'tp')), may hold values from -6 to 6
- expert_ids: int32 [8192, 8], P('grp'), may hold values from 0 to 63, all different within a row; in each aligned block of 128 rows (0 to 127, 128 to 255, ...) at most 24 rows name the same one
- route_logits: float32 [8192, 8], P('grp'), may hold values from -6 to 6
- up_weight: bfloat16 [64, 7168, 1024], P('grp', ('role', 'tp')), may hold values from -0.0625 to 0.0625
- down_weight: bfloat16 [64, 1024, 7168], P('grp', None, ('role', 'tp')), may hold values from -0.1875 to 0.1875
Outputs:
- attn_context: bfloat16 [256, 128, 512], P(('role', 'grp'), 'tp')
- moe_output: bfloat16 [8192, 7168], P('grp', ('role', 'tp'))
The draws below stay inside these ranges and needn't reach their ends.
Inputs may be any that keep to these rules, and one draw needn't show every extreme that they name: `cache_lengths`: each request has 2 to 1024 cached positions; some request has exactly 1024. `expert_ids`: each row names 8 different experts; among the rows of one batch shard no expert is named more than 24 times, a bound that some block reaches.
All inputs are finite; a program needn't handle non-finite values.
Results may differ from the reference program's by a relative error of at most 0.025.
Values may be sent and summed in bfloat16 or wider, within the bound.
No kernel may reach another device: no remote copies, remote signals or barrier semaphores. Data moves between devices by JAX's collectives and lax.ppermute only.
A program may use at most 64 MiB of HBM per device.

```python
import math
import jax
import jax.numpy as jnp
import numpy as np
from jax import lax

D = 7168
HEADS = 128
KEY_VALUE_LATENT = 512
ROPE = 64
QK_NOPE = 128
TOP = 8
FF = 1024
EXPERTS = 64
ROWS_GRP = 128
CAP = 24
LATENT = 576
LMAX = 1024
REQUESTS = 256
ROWS = 8192
N_GRP = 64


def draw_key_value_cache(key, part):
    own_key = jax.random.fold_in(key, 3)
    values = jnp.clip(jax.random.normal(own_key, (REQUESTS, LMAX, LATENT), jnp.float32), -6.0, 6.0)
    return values.astype(jnp.bfloat16)


def draw_q_latent(key, part):
    own_key = jax.random.fold_in(key, 7)
    values = jnp.clip(jax.random.normal(own_key, (REQUESTS, HEADS, LATENT), jnp.float32), -6.0, 6.0)
    return values.astype(jnp.bfloat16)


def draw_cache_lengths(key, part):
    own_key = jax.random.fold_in(key, 5)
    key_a, key_b = jax.random.split(own_key)
    draw_one = jax.random.randint(key_a, (REQUESTS,), 2, LMAX + 1, jnp.int32)
    draw_two = jax.random.randint(key_b, (REQUESTS,), 2, LMAX + 1, jnp.int32)
    lengths = jnp.minimum(draw_one, draw_two)
    return lengths.at[0].set(LMAX)


def levels(rng, shape, shards, low, high):
    def one(position, shards_of):
        heights = jax.random.uniform(jax.random.fold_in(jax.random.fold_in(rng, 6), position), (shards_of,), jnp.float32, low / len(shards), high / len(shards))
        return jnp.repeat(jnp.exp(heights), shape[position] // shards_of).reshape((-1,) + (1,) * (len(shape) - position - 1))

    gain = one(*shards[0])
    for cut in shards[1:]:
        gain = gain * one(*cut)
    return gain


def assign_block(stream_key, own, number, rows, number_of, top, most, skew):
    order = jax.random.permutation(stream_key, number_of)
    heavy_load, ordinary = shares(number_of, rows * top, most, skew, True), shares(number_of, rows * top, most, skew, False)
    places = jnp.arange(number_of)

    def named(sizes, offset_by):
        used = int((sizes > 0).sum())
        fixed = max(1, used // 4)
        passed = fixed + (places - fixed + offset_by * (used - fixed)) % max(1, number_of - fixed)
        return jnp.zeros((number_of,), jnp.int32).at[order[jnp.where(places < fixed, places, passed)]].set(jnp.asarray(sizes, jnp.int32))

    sizes = jnp.where(number % 4 == 0, named(heavy_load, number // 4), named(ordinary, number - number // 4 - 1))
    mixed = jax.random.permutation(jax.random.fold_in(own, 3), number_of)
    giver, receiver = mixed[0:number_of // 2 * 2:2], mixed[1:number_of // 2 * 2:2]
    slack = jnp.minimum(sizes[giver] - 1, most - sizes[receiver]) // 2
    slack = jnp.where((giver == order[0]) | (receiver == order[0]) | (sizes[receiver] == 0), 0, jnp.maximum(slack, 0))
    passed = jax.random.randint(jax.random.fold_in(own, 4), (number_of // 2,), 0, 1 << 20) % (slack + 1)
    sizes = sizes.at[giver].add(-passed).at[receiver].add(passed)
    labels = jnp.searchsorted(jnp.cumsum(sizes), jnp.arange(rows * top), side="right").astype(jnp.int32)
    table = labels.reshape(top, rows).T
    table = table[jax.random.permutation(jax.random.fold_in(own, 1), rows)]
    offset_by = jax.random.randint(jax.random.fold_in(own, 2), (rows, 1), 0, top)
    return jnp.take_along_axis(table, (jnp.arange(top)[None, :] + offset_by) % top, axis=1)


def shares(count, total, bound, lean, full):
    loads = [(1 << 20) // math.isqrt(rank ** lean) + 1 for rank in range(1, count + 1)]
    largest = bound if full else min(bound, max(-(-total // count), total * loads[0] // sum(loads)))
    least = 1 if total - largest >= count - 1 else 0
    given, surplus = [largest] + [least] * (count - 1), total - largest - least * (count - 1)
    while surplus > 0:
        candidates = [i for i in range(1, count) if given[i] < largest] or [i for i in range(1, count) if given[i] < bound]
        whole, remaining = sum([loads[i] for i in candidates]), surplus
        for i in candidates:
            more = min(bound - given[i], max(1, remaining * loads[i] // whole), surplus)
            given[i] = given[i] + more
            surplus = surplus - more
    return np.array(given)


def gaussian(key, shape, deviation, bound, cuts=(), kind=jnp.bfloat16):
    gain = levels(key, shape, cuts, -0.22, 0.18) if cuts else 1.0
    entries = jax.random.normal(key, shape, jnp.float32) * deviation * gain
    return jnp.minimum(jnp.maximum(entries, -bound), bound).astype(kind)


def setup_inputs(seed: int = 0) -> dict:
    key_of = jax.random.split(jax.random.key(seed), 9)
    q_latent = draw_q_latent(jax.random.fold_in(key_of[8], 71), 0)
    key_value_cache = draw_key_value_cache(jax.random.fold_in(key_of[8], 71), 0)
    cache_lengths = draw_cache_lengths(jax.random.fold_in(key_of[8], 71), 0)
    hidden = gaussian(key_of[3], (ROWS, D), 1.0, 6.0, ((0, 64), (1, 8)))
    expert_ids_keys = jax.random.split(jax.random.fold_in(key_of[4], 1), ROWS // ROWS_GRP)
    expert_ids_turns = jax.random.permutation(jax.random.fold_in(key_of[4], 3), ROWS // ROWS_GRP)
    expert_ids = jax.vmap(lambda own, number: assign_block(jax.random.fold_in(key_of[4], 2), own, number, ROWS_GRP, EXPERTS, TOP, CAP, 2))(expert_ids_keys, expert_ids_turns).reshape((ROWS, TOP))
    route_logits = gaussian(key_of[5], (ROWS, TOP), 1.5, 6.0, ((0, 64),), jnp.float32)
    up_weight = gaussian(key_of[6], (EXPERTS, D, FF), D ** -0.5, 0.0625, ((0, 64), (1, 8)))
    down_weight = gaussian(key_of[7], (EXPERTS, FF, D), FF ** -0.5, 0.1875, ((0, 64), (2, 8)))
    return {"q_latent": q_latent, "key_value_cache": key_value_cache, "cache_lengths": cache_lengths, "hidden": hidden, "expert_ids": expert_ids, "route_logits": route_logits, "up_weight": up_weight, "down_weight": down_weight}


NEGATIVE = -1.0e30


def block_ranks(id_rows, rows_block, experts):
    blocks = id_rows.reshape(-1, rows_block * id_rows.shape[1])
    onehot = (blocks[:, :, None] == jnp.arange(experts, dtype=jnp.int32)[None, None, :]).astype(jnp.int32)
    before = jnp.cumsum(onehot, axis=1) - onehot
    return jnp.sum(before * onehot, axis=2).reshape(id_rows.shape).astype(jnp.int32)


def reference(q_latent, key_value_cache, cache_lengths, hidden, expert_ids, route_logits, up_weight, down_weight):
    score_scale = 1.0 / ((QK_NOPE + ROPE) ** 0.5)
    query_f = q_latent.astype(jnp.float32)
    cache_float = key_value_cache.astype(jnp.float32)
    scores = jnp.einsum('rhc,rlc->rhl', query_f, cache_float) * score_scale
    positions = jnp.arange(LMAX, dtype=jnp.int32)
    is_valid = positions[None, None, :] < cache_lengths[:, None, None]
    scores = jnp.where(is_valid, scores, NEGATIVE)
    row_peak = jnp.max(scores, axis=-1)
    exp_terms = jnp.where(is_valid, jnp.exp(scores - row_peak[..., None]), 0.0)
    row_total = jnp.sum(exp_terms, axis=-1)
    exponent_rounded = exp_terms.astype(jnp.bfloat16)
    context_total = jnp.einsum('wzj,wjp->wzp', exponent_rounded.astype(jnp.float32), cache_float[:, :, :KEY_VALUE_LATENT])
    attn_context = (context_total / row_total[..., None]).astype(jnp.bfloat16)

    slot_rank = block_ranks(expert_ids, ROWS_GRP, EXPERTS)
    shard_of = (jnp.arange(ROWS, dtype=jnp.int32) // ROWS_GRP)[:, None]
    slot_index = (shard_of * CAP + slot_rank).astype(jnp.int32)
    row_numbers = jnp.broadcast_to(jnp.arange(ROWS, dtype=jnp.int32)[:, None], expert_ids.shape)
    slots_each = N_GRP * CAP
    table = jnp.zeros((EXPERTS, slots_each), jnp.int32).at[expert_ids, slot_index].set(row_numbers)
    filled = jnp.zeros((EXPERTS, slots_each), jnp.bool_).at[expert_ids, slot_index].set(True)

    def per_expert(expert):
        chosen = hidden[table[expert]]
        expert_input = jnp.where(filled[expert][:, None], chosen, jnp.zeros((), hidden.dtype))
        pre_act = jnp.dot(expert_input, up_weight[expert], preferred_element_type=jnp.float32)
        activation = jax.nn.silu(pre_act).astype(jnp.bfloat16)
        return jnp.dot(activation, down_weight[expert], preferred_element_type=jnp.float32).astype(jnp.bfloat16)

    expert_output = lax.map(per_expert, jnp.arange(EXPERTS, dtype=jnp.int32))
    picked = expert_output[expert_ids, slot_index]
    sigmoid_terms = jax.nn.sigmoid(route_logits)
    route_weights = 2.5 * sigmoid_terms / jnp.sum(sigmoid_terms, axis=-1, keepdims=True)
    moe_output = jnp.sum(route_weights[:, :, None] * picked.astype(jnp.float32), axis=1).astype(jnp.bfloat16)
    return attn_context, moe_output
```

```python
import jax
import jax.numpy as jnp
from jax import lax
from jax.sharding import PartitionSpec as P

KEY_VALUE_LATENT = 512
ROPE = 64
QK_NOPE = 128
EXPERTS = 64
CAP = 24
PARTS = ((0, 16), (16, 24))
LANES = 128

NEGATIVE = -1e30


def two_halves(value):
    high = value.astype(jnp.bfloat16)
    low = (value - high.astype(jnp.float32)).astype(jnp.bfloat16)
    return high, low


def attention_part(q_latent, key_value_cache, cache_lengths):
    score_scale = 1.0 / (QK_NOPE + ROPE) ** 0.5
    local_len = key_value_cache.shape[1]
    offset = lax.axis_index("tp") * local_len
    positions = offset + jnp.arange(local_len, dtype=jnp.int32)
    is_valid = positions[None, None, :] < cache_lengths[:, None, None]
    scores = (
        jnp.einsum("rhc,rlc->rhl", q_latent, key_value_cache, preferred_element_type=jnp.float32)
        * score_scale
    )
    scores = jnp.where(is_valid, scores, NEGATIVE)
    shift = jnp.max(scores, axis=-1).astype(jnp.bfloat16)
    exp_terms = jnp.where(
        is_valid, jnp.exp(scores - shift.astype(jnp.float32)[..., None]), 0.0
    )
    row_total = jnp.sum(exp_terms, axis=-1)
    context_total = jnp.einsum(
        "wzj,wjp->wzp",
        exp_terms.astype(jnp.bfloat16),
        key_value_cache[:, :, :KEY_VALUE_LATENT],
        preferred_element_type=jnp.float32,
    )
    total_high, total_low = two_halves(row_total)
    stats = jnp.stack([shift, total_high, total_low], axis=-1)
    stats = jnp.pad(stats, ((0, 0), (0, 0), (0, LANES - stats.shape[-1])))
    return jnp.concatenate([context_total.astype(jnp.bfloat16), stats], axis=-1)


def attention_join(everything, head_group):
    first = lax.axis_index("tp") * head_group
    mine = lax.dynamic_slice_in_dim(everything, first, head_group, 2)
    mine = lax.optimization_barrier(mine)
    context = mine[..., :KEY_VALUE_LATENT].astype(jnp.float32)
    stats = mine[..., KEY_VALUE_LATENT : KEY_VALUE_LATENT + 3].astype(jnp.float32)
    shift = stats[..., 0]
    total = stats[..., 1] + stats[..., 2]
    factor = jnp.exp(shift - jnp.max(shift, axis=0, keepdims=True))
    total_all = jnp.sum(total * factor, axis=0)
    context_all = jnp.sum(context * factor[..., None], axis=0)
    return (context_all / total_all[..., None]).astype(jnp.bfloat16)


def turned(value, axis, step):
    size = lax.axis_size(axis)
    return lax.ppermute(value, axis, [(k, (k + step) % size) for k in range(size)])


def summed_products(rows_in, weight):
    role = lax.axis_index("role")
    place = lax.axis_index("tp")
    size = lax.axis_size("tp")
    half = rows_in.shape[0] // 2
    share = half // size
    theirs = lax.dynamic_slice_in_dim(rows_in, (1 - role) * half, half, 0)
    mine = lax.dynamic_slice_in_dim(rows_in, role * half, half, 0)
    sent = jnp.dot(theirs, weight, preferred_element_type=jnp.float32).astype(jnp.bfloat16)
    arrived = turned(sent, "role", 1)
    total = jnp.dot(mine, weight, preferred_element_type=jnp.float32) + arrived.astype(jnp.float32)
    rounded = total.astype(jnp.bfloat16)
    shares = []
    for step in (2, 1, 3):
        piece = lax.dynamic_slice_in_dim(rounded, (place + step) % size * share, share, 0)
        shares.append(turned(piece, "tp", step))
    own = lax.dynamic_slice_in_dim(total, place * share, share, 0)
    for piece in shares:
        own = own + piece.astype(jnp.float32)
    return own


def spread(value, rows_all):
    place = lax.axis_index("tp")
    size = lax.axis_size("tp")
    share = value.shape[0]
    half = jnp.zeros((rows_all // 2, value.shape[1]), value.dtype)
    half = lax.dynamic_update_slice_in_dim(half, value, place * share, 0)
    for step in (2, 1, 3):
        piece = turned(value, "tp", step)
        half = lax.dynamic_update_slice_in_dim(half, piece, (place - step) % size * share, 0)
    return half, turned(half, "role", 1)


def shards(
    q_latent,
    key_value_cache,
    cache_lengths,
    hidden,
    expert_ids,
    route_logits,
    up_weight,
    down_weight,
):
    rows, width = hidden.shape
    owners = lax.axis_size("grp")
    role = lax.axis_index("role")
    experts = jnp.arange(EXPERTS, dtype=jnp.int32)
    up = up_weight[0]
    down = down_weight[0]

    named = expert_ids[:, None, :] == experts[None, :, None]
    named_any = jnp.any(named, axis=2)
    row_numbers = jnp.arange(rows, dtype=jnp.int32)
    lower = (row_numbers[None, :] < row_numbers[:, None]).astype(jnp.bfloat16)
    before = jnp.dot(
        lower, named_any.astype(jnp.bfloat16), preferred_element_type=jnp.float32
    ).astype(jnp.int32)
    rank = jnp.where(named_any, before, -1)
    rank_by_expert = rank.T

    arrivals = []
    for first, last in PARTS:
        slots = jnp.arange(first, last, dtype=jnp.int32)
        placed = rank_by_expert[:, None, :] == slots[None, :, None]
        placed = placed.reshape(-1, rows).astype(jnp.bfloat16)
        outgoing = jnp.dot(placed, hidden, preferred_element_type=jnp.float32).astype(jnp.bfloat16)
        if arrivals:
            outgoing, arrivals[-1] = lax.optimization_barrier((outgoing, arrivals[-1]))
        arrivals.append(
            lax.all_to_all(
                outgoing.reshape(owners, last - first, width),
                "grp",
                split_axis=0,
                concat_axis=0,
                tiled=True,
            )
        )

    packed = attention_part(q_latent, key_value_cache, cache_lengths)
    everything = lax.all_gather(packed, "tp")
    attn_context = attention_join(everything, q_latent.shape[1] // lax.axis_size("tp"))

    sigmoid_terms = jax.nn.sigmoid(route_logits)
    route_weights = 2.5 * sigmoid_terms / jnp.sum(sigmoid_terms, axis=-1, keepdims=True)
    weight_of = jnp.sum(jnp.where(named, route_weights[:, None, :], 0.0), axis=2)

    result = jnp.zeros((2 * rows, width), jnp.float32)
    earlier = None
    for (first, last), incoming in zip(PARTS, arrivals):
        slots = jnp.arange(first, last, dtype=jnp.int32)
        count = owners * (last - first)
        if earlier is not None:
            incoming, _ = lax.optimization_barrier((incoming, earlier))
        own = summed_products(incoming.reshape(count, width), up)
        activated = jax.nn.silu(own).astype(jnp.bfloat16)
        produced = jnp.zeros((count, width), jnp.bfloat16)
        halves = spread(activated, count)
        for which, half in zip((role, 1 - role), halves):
            out = jnp.dot(half, down, preferred_element_type=jnp.float32).astype(jnp.bfloat16)
            produced = lax.dynamic_update_slice_in_dim(produced, out, which * (count // 2), 0)
        earlier = produced
        returned = lax.all_to_all(
            produced.reshape(owners, last - first, width),
            "grp",
            split_axis=0,
            concat_axis=0,
            tiled=True,
        )
        taken = rank[:, :, None] == slots[None, None, :]
        weights = jnp.where(taken, weight_of[:, :, None], 0.0).reshape(rows, -1)
        both = jnp.concatenate(two_halves(weights), axis=0)
        result = result + jnp.dot(
            both, returned.reshape(count, width), preferred_element_type=jnp.float32
        )
    moe_output = (result[:rows] + result[rows:]).astype(jnp.bfloat16)
    return (attn_context, moe_output)


def solution(mesh):
    return jax.shard_map(
        shards,
        mesh=mesh,
        in_specs=(
            P(("role", "grp"), None, None),
            P(("role", "grp"), "tp", None),
            P(("role", "grp")),
            P("grp", ("role", "tp")),
            P("grp", None),
            P("grp", None),
            P("grp", ("role", "tp"), None),
            P("grp", None, ("role", "tp")),
        ),
        out_specs=(P(("role", "grp"), "tp", None), P("grp", ("role", "tp"))),
        check_vma=False,
    )
```

```python
import functools

import jax
import jax.numpy as jnp
from jax import lax
from jax.experimental import pallas as pl
from jax.experimental.pallas import tpu as pltpu
from jax.sharding import PartitionSpec as P

KEY_VALUE_LATENT = 512
ROPE = 64
QK_NOPE = 128
EXPERTS = 64
CAP = 24
PARTS = ((0, 8), (8, 24))
VMEM = 40 * 1024 * 1024
LANES = 128

NEGATIVE = -1e30


def two_halves(value):
    high = value.astype(jnp.bfloat16)
    low = (value - high.astype(jnp.float32)).astype(jnp.bfloat16)
    return high, low


def attention_part(q_latent, key_value_cache, cache_lengths):
    score_scale = 1.0 / (QK_NOPE + ROPE) ** 0.5
    local_len = key_value_cache.shape[1]
    offset = lax.axis_index("tp") * local_len
    positions = offset + jnp.arange(local_len, dtype=jnp.int32)
    is_valid = positions[None, None, :] < cache_lengths[:, None, None]
    scores = (
        jnp.einsum("rhc,rlc->rhl", q_latent, key_value_cache, preferred_element_type=jnp.float32)
        * score_scale
    )
    scores = jnp.where(is_valid, scores, NEGATIVE)
    shift = jnp.max(scores, axis=-1).astype(jnp.bfloat16)
    exp_terms = jnp.where(
        is_valid, jnp.exp(scores - shift.astype(jnp.float32)[..., None]), 0.0
    )
    row_total = jnp.sum(exp_terms, axis=-1)
    context_total = jnp.einsum(
        "wzj,wjp->wzp",
        exp_terms.astype(jnp.bfloat16),
        key_value_cache[:, :, :KEY_VALUE_LATENT],
        preferred_element_type=jnp.float32,
    )
    total_high, total_low = two_halves(row_total)
    stats = jnp.stack([shift, total_high, total_low], axis=-1)
    stats = jnp.pad(stats, ((0, 0), (0, 0), (0, LANES - stats.shape[-1])))
    return jnp.concatenate([context_total.astype(jnp.bfloat16), stats], axis=-1)


def attention_join(everything, head_group):
    first = lax.axis_index("tp") * head_group
    mine = lax.dynamic_slice_in_dim(everything, first, head_group, 2)
    mine = lax.optimization_barrier(mine)
    context = mine[..., :KEY_VALUE_LATENT].astype(jnp.float32)
    stats = mine[..., KEY_VALUE_LATENT : KEY_VALUE_LATENT + 3].astype(jnp.float32)
    shift = stats[..., 0]
    total = stats[..., 1] + stats[..., 2]
    factor = jnp.exp(shift - jnp.max(shift, axis=0, keepdims=True))
    total_all = jnp.sum(total * factor, axis=0)
    context_all = jnp.sum(context * factor[..., None], axis=0)
    return (context_all / total_all[..., None]).astype(jnp.bfloat16)


def turned(value, axis, step):
    size = lax.axis_size(axis)
    return lax.ppermute(value, axis, [(k, (k + step) % size) for k in range(size)])


def cost(rows, depth, columns):
    return pl.CostEstimate(
        flops=2 * rows * depth * columns,
        bytes_accessed=2 * (rows * depth + depth * columns + rows * columns),
        transcendentals=0,
    )


def their_kernel(where, rows_ref, weight_ref, out_ref):
    out_ref[...] = jnp.dot(
        rows_ref[...], weight_ref[...], preferred_element_type=jnp.float32
    ).astype(out_ref.dtype)


def their_half(where, rows_in, weight):
    half, depth = rows_in.shape[0] // 2, rows_in.shape[1]
    columns = weight.shape[1]
    tile = min(256, half)
    steps = half // tile
    return pl.pallas_call(
        their_kernel,
        out_shape=jax.ShapeDtypeStruct((half, columns), jnp.bfloat16),
        grid_spec=pltpu.PrefetchScalarGridSpec(
            num_scalar_prefetch=1,
            grid=(steps,),
            in_specs=[
                pl.BlockSpec((tile, depth), lambda i, where: ((1 - where[0]) * steps + i, 0)),
                pl.BlockSpec((depth, columns), lambda i, where: (0, 0)),
            ],
            out_specs=pl.BlockSpec((tile, columns), lambda i, where: (i, 0)),
        ),
        compiler_params=pltpu.CompilerParams(vmem_limit_bytes=VMEM),
        cost_estimate=cost(half, depth, columns),
        name="their_half",
    )(where, rows_in, weight)


def own_kernel(where, rows_ref, weight_ref, arrived_ref, own_ref, *rest):
    piece_refs, total = rest[:-1], rest[-1]
    tile = rows_ref.shape[0]
    share = own_ref.shape[0]
    size = total.shape[0] // share
    step = pl.program_id(0)
    here = pl.ds(pl.multiple_of(step * tile, tile), tile)
    total[here, :] = jnp.dot(
        rows_ref[...], weight_ref[...], preferred_element_type=jnp.float32
    ) + arrived_ref[...].astype(jnp.float32)

    @pl.when(step == pl.num_programs(0) - 1)
    def _():
        if size == 1:
            own_ref[...] = total[...]
            piece_refs[0][...] = total[...].astype(jnp.bfloat16)
        else:
            for ahead in range(size):
                place = lax.rem(where[1] + ahead, size)
                piece = total[pl.ds(pl.multiple_of(place * share, share), share), :]
                if ahead == 0:
                    own_ref[...] = piece
                else:
                    piece_refs[ahead - 1][...] = piece.astype(jnp.bfloat16)


def own_half(where, rows_in, weight, arrived, size):
    half, depth = rows_in.shape[0] // 2, rows_in.shape[1]
    columns = weight.shape[1]
    tile = min(256, half)
    steps = half // tile
    share = half // size
    return pl.pallas_call(
        own_kernel,
        out_shape=[jax.ShapeDtypeStruct((share, columns), jnp.float32)]
        + [jax.ShapeDtypeStruct((share, columns), jnp.bfloat16)] * max(1, size - 1),
        grid_spec=pltpu.PrefetchScalarGridSpec(
            num_scalar_prefetch=1,
            grid=(steps,),
            in_specs=[
                pl.BlockSpec((tile, depth), lambda i, where: (where[0] * steps + i, 0)),
                pl.BlockSpec((depth, columns), lambda i, where: (0, 0)),
                pl.BlockSpec((tile, columns), lambda i, where: (i, 0)),
            ],
            out_specs=[pl.BlockSpec((share, columns), lambda i, where: (0, 0))]
            * max(2, size),
            scratch_shapes=[pltpu.VMEM((half, columns), jnp.float32)],
        ),
        compiler_params=pltpu.CompilerParams(vmem_limit_bytes=VMEM),
        cost_estimate=cost(half, depth, columns),
        name="own_half",
    )(where, rows_in, weight, arrived)


def down_kernel(where, mine_ref, theirs_ref, weight_ref, out_ref):
    @pl.when(pl.program_id(0) == 0)
    def _():
        out_ref[...] = jnp.dot(
            mine_ref[...], weight_ref[...], preferred_element_type=jnp.float32
        ).astype(out_ref.dtype)

    @pl.when(pl.program_id(0) == 1)
    def _():
        out_ref[...] = jnp.dot(
            theirs_ref[...], weight_ref[...], preferred_element_type=jnp.float32
        ).astype(out_ref.dtype)


def down_both(where, mine, theirs, weight, size):
    half, depth = mine.shape
    columns = weight.shape[1]
    share = half // size

    def place(core, back, where):
        which = where[0] + core - 2 * where[0] * core
        return which * size + lax.rem(where[1] * (size > 1) + size - back, size), 0

    return pl.pallas_call(
        down_kernel,
        out_shape=jax.ShapeDtypeStruct((2 * half, columns), jnp.bfloat16),
        grid_spec=pltpu.PrefetchScalarGridSpec(
            num_scalar_prefetch=1,
            grid=(2, size),
            in_specs=[
                pl.BlockSpec((share, depth), lambda h, i, where: (i * (1 - h) + (size - 1) * h, 0)),
                pl.BlockSpec((share, depth), lambda h, i, where: (i * h, 0)),
                pl.BlockSpec((depth, columns), lambda h, i, where: (0, 0)),
            ],
            out_specs=pl.BlockSpec((share, columns), place),
        ),
        compiler_params=pltpu.CompilerParams(vmem_limit_bytes=VMEM),
        cost_estimate=cost(2 * half, depth, columns),
        name="down_both",
    )(where, mine, theirs, weight)


def expert_rows(where, rows_in, up, down, one_step):
    size = lax.axis_size("tp")
    arrived = turned(their_half(where, rows_in, up), "role", 1)
    if one_step:
        own, rounded = own_half(where, rows_in, up, arrived, 1)
        pieces = [turned(rounded, "tp", step) for step in (2, 1, 3)]
    else:
        own, *pieces = own_half(where, rows_in, up, arrived, size)
        pieces = [turned(pieces[step - 1], "tp", step) for step in (2, 1, 3)]
    for piece in pieces:
        own = own + piece.astype(jnp.float32)
    mine = jax.nn.silu(own).astype(jnp.bfloat16)
    if not one_step:
        others = {step: turned(mine, "tp", step) for step in (2, 1, 3)}
        mine = jnp.concatenate([mine] + [others[step] for step in range(1, size)], axis=0)
    theirs = turned(mine, "role", 1)
    return down_both(where, mine, theirs, down, 1 if one_step else size)


def shards(
    q_latent,
    key_value_cache,
    cache_lengths,
    hidden,
    expert_ids,
    route_logits,
    up_weight,
    down_weight,
):
    rows, width = hidden.shape
    owners = lax.axis_size("grp")
    experts = jnp.arange(EXPERTS, dtype=jnp.int32)
    where = jnp.stack([lax.axis_index("role"), lax.axis_index("tp")]).astype(jnp.int32)
    up = up_weight[0]
    down = down_weight[0]

    named = expert_ids[:, None, :] == experts[None, :, None]
    named_any = jnp.any(named, axis=2)
    row_numbers = jnp.arange(rows, dtype=jnp.int32)
    lower = (row_numbers[None, :] < row_numbers[:, None]).astype(jnp.bfloat16)
    before = jnp.dot(
        lower, named_any.astype(jnp.bfloat16), preferred_element_type=jnp.float32
    ).astype(jnp.int32)
    rank = jnp.where(named_any, before, -1)
    rank_by_expert = rank.T

    def exchanged(value, count):
        return lax.all_to_all(
            value.reshape(owners, count, width), "grp", split_axis=0, concat_axis=0, tiled=True
        ).reshape(owners * count, width)

    def outgoing(part):
        slots = jnp.arange(*part, dtype=jnp.int32)
        placed = rank_by_expert[:, None, :] == slots[None, :, None]
        placed = placed.reshape(-1, rows).astype(jnp.bfloat16)
        return jnp.dot(placed, hidden, preferred_element_type=jnp.float32).astype(jnp.bfloat16)

    def weights(part):
        slots = jnp.arange(*part, dtype=jnp.int32)
        taken = rank[:, :, None] == slots[None, None, :]
        return jnp.concatenate(
            two_halves(jnp.where(taken, weight_of[:, :, None], 0.0).reshape(rows, -1)), axis=0
        )

    counts = [last - first for first, last in PARTS]
    first_in = exchanged(outgoing(PARTS[0]), counts[0])

    packed = attention_part(q_latent, key_value_cache, cache_lengths)
    everything = lax.all_gather(packed, "tp")

    sigmoid_terms = jax.nn.sigmoid(route_logits)
    route_weights = 2.5 * sigmoid_terms / jnp.sum(sigmoid_terms, axis=-1, keepdims=True)
    weight_of = jnp.sum(jnp.where(named, route_weights[:, None, :], 0.0), axis=2)
    weights_of = [weights(part) for part in PARTS]

    second_out, first_in, *weights_of, packed = lax.optimization_barrier(
        (outgoing(PARTS[1]), first_in, *weights_of, packed)
    )
    second_in = exchanged(second_out, counts[1])
    first_out = expert_rows(where, first_in, up, down, True)
    second_in, first_out = lax.optimization_barrier((second_in, first_out))
    first_back = exchanged(first_out, counts[0])
    second_out = expert_rows(where, second_in, up, down, False)
    second_back = exchanged(second_out, counts[1])

    everything, second_out = lax.optimization_barrier((everything, second_out))
    attn_context = attention_join(everything, q_latent.shape[1] // lax.axis_size("tp"))
    result = jnp.dot(weights_of[0], first_back, preferred_element_type=jnp.float32)
    result = result + jnp.dot(weights_of[1], second_back, preferred_element_type=jnp.float32)
    moe_output = (result[:rows] + result[rows:]).astype(jnp.bfloat16)
    return (attn_context, moe_output)


def solution(mesh):
    return jax.shard_map(
        shards,
        mesh=mesh,
        in_specs=(
            P(("role", "grp"), None, None),
            P(("role", "grp"), "tp", None),
            P(("role", "grp")),
            P("grp", ("role", "tp")),
            P("grp", None),
            P("grp", None),
            P("grp", ("role", "tp"), None),
            P("grp", None, ("role", "tp")),
        ),
        out_specs=(P(("role", "grp"), "tp", None), P("grp", ("role", "tp"))),
        check_vma=False,
    )
```

```python
import functools

import jax
import jax.numpy as jnp
from jax import lax
from jax.experimental import pallas as pl
from jax.experimental.pallas import tpu as pltpu
from jax.sharding import PartitionSpec as P

KEY_VALUE_LATENT = 512
ROPE = 64
QK_NOPE = 128
EXPERTS = 64
CAP = 24
FIRST = 8
VMEM = 32 * 1024 * 1024
LANES = 128

NEGATIVE = -1e30


def two_halves(value):
    high = value.astype(jnp.bfloat16)
    low = (value - high.astype(jnp.float32)).astype(jnp.bfloat16)
    return high, low


def attention_part(q_latent, key_value_cache, cache_lengths):
    score_scale = 1.0 / (QK_NOPE + ROPE) ** 0.5
    local_len = key_value_cache.shape[1]
    offset = lax.axis_index("tp") * local_len
    positions = offset + jnp.arange(local_len, dtype=jnp.int32)
    is_valid = positions[None, None, :] < cache_lengths[:, None, None]
    scores = (
        jnp.einsum("rhc,rlc->rhl", q_latent, key_value_cache, preferred_element_type=jnp.float32)
        * score_scale
    )
    scores = jnp.where(is_valid, scores, NEGATIVE)
    shift = jnp.max(scores, axis=-1).astype(jnp.bfloat16)
    exp_terms = jnp.where(
        is_valid, jnp.exp(scores - shift.astype(jnp.float32)[..., None]), 0.0
    )
    row_total = jnp.sum(exp_terms, axis=-1)
    context_total = jnp.einsum(
        "wzj,wjp->wzp",
        exp_terms.astype(jnp.bfloat16),
        key_value_cache[:, :, :KEY_VALUE_LATENT],
        preferred_element_type=jnp.float32,
    )
    total_high, total_low = two_halves(row_total)
    stats = jnp.stack([shift, total_high, total_low], axis=-1)
    stats = jnp.pad(stats, ((0, 0), (0, 0), (0, LANES - stats.shape[-1])))
    return jnp.concatenate([context_total.astype(jnp.bfloat16), stats], axis=-1)


def attention_join(pieces):
    mine = jnp.stack(pieces)
    context = mine[..., :KEY_VALUE_LATENT].astype(jnp.float32)
    stats = mine[..., KEY_VALUE_LATENT : KEY_VALUE_LATENT + 3].astype(jnp.float32)
    shift = stats[..., 0]
    total = stats[..., 1] + stats[..., 2]
    factor = jnp.exp(shift - jnp.max(shift, axis=0, keepdims=True))
    total_all = jnp.sum(total * factor, axis=0)
    context_all = jnp.sum(context * factor[..., None], axis=0)
    return (context_all / total_all[..., None]).astype(jnp.bfloat16)


def turned(value, axis, step):
    size = lax.axis_size(axis)
    return lax.ppermute(value, axis, [(k, (k + step) % size) for k in range(size)])


def cost(rows, depth, columns):
    return pl.CostEstimate(
        flops=2 * rows * depth * columns,
        bytes_accessed=2 * (rows * depth + depth * columns + rows * columns),
        transcendentals=0,
    )


def their_kernel(where, rows_ref, weight_ref, out_ref):
    out_ref[...] = jnp.dot(
        rows_ref[...], weight_ref[...], preferred_element_type=jnp.float32
    ).astype(out_ref.dtype)


def their_half(where, rows_in, weight):
    half, depth = rows_in.shape[0] // 2, rows_in.shape[1]
    columns = weight.shape[1]
    tile = min(256, half)
    steps = half // tile
    return pl.pallas_call(
        their_kernel,
        out_shape=jax.ShapeDtypeStruct((half, columns), jnp.bfloat16),
        grid_spec=pltpu.PrefetchScalarGridSpec(
            num_scalar_prefetch=1,
            grid=(steps,),
            in_specs=[
                pl.BlockSpec((tile, depth), lambda i, where: ((1 - where[0]) * steps + i, 0)),
                pl.BlockSpec((depth, columns), lambda i, where: (0, 0)),
            ],
            out_specs=pl.BlockSpec((tile, columns), lambda i, where: (i, 0)),
        ),
        compiler_params=pltpu.CompilerParams(vmem_limit_bytes=VMEM),
        cost_estimate=cost(half, depth, columns),
        name="their_half",
    )(where, rows_in, weight)


def own_kernel(where, rows_ref, weight_ref, arrived_ref, own_ref, *rest):
    piece_refs, total = rest[:-1], rest[-1]
    tile = rows_ref.shape[0]
    share = own_ref.shape[0]
    size = total.shape[0] // share
    step = pl.program_id(0)
    here = pl.ds(pl.multiple_of(step * tile, tile), tile)
    total[here, :] = jnp.dot(
        rows_ref[...], weight_ref[...], preferred_element_type=jnp.float32
    ) + arrived_ref[...].astype(jnp.float32)

    @pl.when(step == pl.num_programs(0) - 1)
    def _():
        if size == 1:
            own_ref[...] = total[...]
            piece_refs[0][...] = total[...].astype(jnp.bfloat16)
        else:
            for ahead in range(size):
                place = lax.rem(where[1] + ahead, size)
                piece = total[pl.ds(pl.multiple_of(place * share, share), share), :]
                if ahead == 0:
                    own_ref[...] = piece
                else:
                    piece_refs[ahead - 1][...] = piece.astype(jnp.bfloat16)


def own_half(where, rows_in, weight, arrived, size):
    half, depth = rows_in.shape[0] // 2, rows_in.shape[1]
    columns = weight.shape[1]
    tile = min(256, half)
    steps = half // tile
    share = half // size
    return pl.pallas_call(
        own_kernel,
        out_shape=[jax.ShapeDtypeStruct((share, columns), jnp.float32)]
        + [jax.ShapeDtypeStruct((share, columns), jnp.bfloat16)] * max(1, size - 1),
        grid_spec=pltpu.PrefetchScalarGridSpec(
            num_scalar_prefetch=1,
            grid=(steps,),
            in_specs=[
                pl.BlockSpec((tile, depth), lambda i, where: (where[0] * steps + i, 0)),
                pl.BlockSpec((depth, columns), lambda i, where: (0, 0)),
                pl.BlockSpec((tile, columns), lambda i, where: (i, 0)),
            ],
            out_specs=[pl.BlockSpec((share, columns), lambda i, where: (0, 0))]
            * max(2, size),
            scratch_shapes=[pltpu.VMEM((half, columns), jnp.float32)],
        ),
        compiler_params=pltpu.CompilerParams(vmem_limit_bytes=VMEM),
        cost_estimate=cost(half, depth, columns),
        name="own_half",
    )(where, rows_in, weight, arrived)


def down_kernel(where, mine_ref, theirs_ref, weight_ref, out_ref):
    @pl.when(pl.program_id(0) == 0)
    def _():
        out_ref[...] = jnp.dot(
            mine_ref[...], weight_ref[...], preferred_element_type=jnp.float32
        ).astype(out_ref.dtype)

    @pl.when(pl.program_id(0) == 1)
    def _():
        out_ref[...] = jnp.dot(
            theirs_ref[...], weight_ref[...], preferred_element_type=jnp.float32
        ).astype(out_ref.dtype)


def down_both(where, mine, theirs, weight, size):
    half, depth = mine.shape
    columns = weight.shape[1]
    share = half // size

    def place(core, back, where):
        which = where[0] + core - 2 * where[0] * core
        return which * size + lax.rem(where[1] * (size > 1) + size - back, size), 0

    return pl.pallas_call(
        down_kernel,
        out_shape=jax.ShapeDtypeStruct((2 * half, columns), jnp.bfloat16),
        grid_spec=pltpu.PrefetchScalarGridSpec(
            num_scalar_prefetch=1,
            grid=(2, size),
            in_specs=[
                pl.BlockSpec((share, depth), lambda h, i, where: (i * (1 - h) + (size - 1) * h, 0)),
                pl.BlockSpec((share, depth), lambda h, i, where: (i * h, 0)),
                pl.BlockSpec((depth, columns), lambda h, i, where: (0, 0)),
            ],
            out_specs=pl.BlockSpec((share, columns), place),
        ),
        compiler_params=pltpu.CompilerParams(vmem_limit_bytes=VMEM),
        cost_estimate=cost(2 * half, depth, columns),
        name="down_both",
    )(where, mine, theirs, weight)


def wide_kernel(where, rows_ref, weight_ref, other_ref, own_ref, *rest):
    piece_refs, total = rest[:-1], rest[-1]
    tile = rows_ref.shape[0]
    depth = weight_ref.shape[0]
    share = own_ref.shape[0]
    size = total.shape[0] // share
    step = pl.program_id(0)
    here = pl.ds(pl.multiple_of(step * tile, tile), tile)
    total[here, :] = jnp.dot(
        rows_ref[:, :depth], weight_ref[...], preferred_element_type=jnp.float32
    ) + jnp.dot(rows_ref[:, depth:], other_ref[...], preferred_element_type=jnp.float32)

    @pl.when(step == pl.num_programs(0) - 1)
    def _():
        for ahead in range(size):
            place = lax.rem(where[1] + ahead, size)
            piece = total[pl.ds(pl.multiple_of(place * share, share), share), :]
            if ahead == 0:
                own_ref[...] = piece
            else:
                piece_refs[ahead - 1][...] = piece.astype(jnp.bfloat16)


def wide_product(where, rows_in, weight, other, size):
    rows, width = rows_in.shape
    depth, columns = weight.shape
    tile = 256
    share = rows // size
    return pl.pallas_call(
        wide_kernel,
        out_shape=[jax.ShapeDtypeStruct((share, columns), jnp.float32)]
        + [jax.ShapeDtypeStruct((share, columns), jnp.bfloat16)] * (size - 1),
        grid_spec=pltpu.PrefetchScalarGridSpec(
            num_scalar_prefetch=1,
            grid=(rows // tile,),
            in_specs=[
                pl.BlockSpec((tile, width), lambda i, where: (i, 0)),
                pl.BlockSpec((depth, columns), lambda i, where: (0, 0)),
                pl.BlockSpec((depth, columns), lambda i, where: (0, 0)),
            ],
            out_specs=[pl.BlockSpec((share, columns), lambda i, where: (0, 0))] * size,
            scratch_shapes=[pltpu.VMEM((rows, columns), jnp.float32)],
        ),
        compiler_params=pltpu.CompilerParams(vmem_limit_bytes=VMEM),
        cost_estimate=cost(rows, width, columns),
        name="wide_product",
    )(where, rows_in, weight, other)


def down_half_kernel(where, rows_ref, weight_ref, *rest):
    out_ref = rest[-1]
    sources, _, slots, columns = out_ref.shape
    size = 4
    share = sources // size
    together = rows_ref.shape[0] // (share * slots)
    made = jnp.dot(rows_ref[...], weight_ref[...], preferred_element_type=jnp.float32)
    for k in range(together):
        back = pl.program_id(0) * together + k
        place = lax.rem(where[1] + size - back, size)
        piece = made[k * share * slots : (k + 1) * share * slots]
        out_ref[pl.ds(place * share, share), 0] = piece.reshape(share, slots, columns).astype(
            out_ref.dtype
        )


def down_half(where, core, rows_in, weight, made, sources):
    rows, depth = rows_in.shape
    columns = weight.shape[1]
    slots = rows // sources
    tile = rows // 2
    in_specs = [
        pl.BlockSpec((tile, depth), lambda i, where: (i, 0)),
        pl.BlockSpec((depth, columns), lambda i, where: (0, 0)),
    ]
    inputs = [rows_in, weight]
    aliases = {}
    if made is not None:
        in_specs.append(pl.BlockSpec(memory_space=pl.ANY))
        inputs.append(made)
        aliases = {3: 0}

    def half(i, where):
        return 0, where[0] + core - 2 * where[0] * core, 0, 0

    return pl.pallas_call(
        down_half_kernel,
        out_shape=jax.ShapeDtypeStruct((sources, 2, slots, columns), jnp.bfloat16),
        grid_spec=pltpu.PrefetchScalarGridSpec(
            num_scalar_prefetch=1,
            grid=(rows // tile,),
            in_specs=in_specs,
            out_specs=pl.BlockSpec((sources, 1, slots, columns), half),
        ),
        input_output_aliases=aliases,
        compiler_params=pltpu.CompilerParams(vmem_limit_bytes=VMEM),
        cost_estimate=cost(rows, depth, columns),
        name="down_half",
    )(where, *inputs)


def narrow_rows(where, rows_in, up, down):
    arrived = turned(their_half(where, rows_in, up), "role", 1)
    own, rounded = own_half(where, rows_in, up, arrived, 1)
    pieces = [turned(rounded, "tp", step) for step in (2, 1, 3)]
    for piece in pieces:
        own = own + piece.astype(jnp.float32)
    mine = jax.nn.silu(own).astype(jnp.bfloat16)
    return down_both(where, mine, turned(mine, "role", 1), down, 1)


def wide_rows(where, rows_in, up, other_up, down, sources):
    size = lax.axis_size("tp")
    own, *pieces = wide_product(where, rows_in, up, other_up, size)
    for step in (2, 1, 3):
        own = own + turned(pieces[step - 1], "tp", step).astype(jnp.float32)
    mine = jax.nn.silu(own).astype(jnp.bfloat16)
    others = {step: turned(mine, "tp", step) for step in (2, 1, 3)}
    mine = jnp.concatenate([mine] + [others[step] for step in range(1, size)], axis=0)
    theirs = turned(mine, "role", 1)
    made = down_half(where, 0, mine, down, None, sources)
    return down_half(where, 1, theirs, down, made, sources)


def shards(
    q_latent,
    key_value_cache,
    cache_lengths,
    hidden,
    expert_ids,
    route_logits,
    up_weight,
    down_weight,
):
    rows, width = hidden.shape
    owners = lax.axis_size("grp")
    experts = jnp.arange(EXPERTS, dtype=jnp.int32)
    where = jnp.stack([lax.axis_index("role"), lax.axis_index("tp")]).astype(jnp.int32)
    up = up_weight[0]
    down = down_weight[0]

    named = expert_ids[:, None, :] == experts[None, :, None]
    named_any = jnp.any(named, axis=2)
    row_numbers = jnp.arange(rows, dtype=jnp.int32)
    lower = (row_numbers[None, :] < row_numbers[:, None]).astype(jnp.bfloat16)
    before = jnp.dot(
        lower, named_any.astype(jnp.bfloat16), preferred_element_type=jnp.float32
    ).astype(jnp.int32)
    rank = jnp.where(named_any, before, -1)
    rank_by_expert = rank.T

    def exchanged(value):
        return lax.all_to_all(value, "grp", split_axis=0, concat_axis=0, tiled=True)

    def outgoing(first, count, source):
        slots = first + jnp.arange(count, dtype=jnp.int32)
        placed = rank_by_expert[:, None, :] == slots[None, :, None]
        placed = placed.reshape(-1, rows).astype(jnp.bfloat16)
        made = jnp.dot(placed, source, preferred_element_type=jnp.float32).astype(jnp.bfloat16)
        return made.reshape(owners, count, source.shape[1])

    def weights(first, last):
        slots = jnp.arange(first, last, dtype=jnp.int32)
        taken = rank[:, :, None] == slots[None, None, :]
        return jnp.concatenate(
            two_halves(jnp.where(taken, weight_of[:, :, None], 0.0).reshape(rows, -1)), axis=0
        )

    first_out = outgoing(0, FIRST, hidden)
    first_out, hidden = lax.optimization_barrier((first_out, hidden))
    first_in = exchanged(first_out)

    wide = jnp.concatenate([hidden, turned(hidden, "role", 1)], axis=1)

    sigmoid_terms = jax.nn.sigmoid(route_logits)
    route_weights = 2.5 * sigmoid_terms / jnp.sum(sigmoid_terms, axis=-1, keepdims=True)
    weight_of = jnp.sum(jnp.where(named, route_weights[:, None, :], 0.0), axis=2)
    weights_of = [weights(0, FIRST), weights(FIRST, CAP)]

    half = (CAP - FIRST) // 2
    begin = FIRST + where[0] * half
    second_out, first_in, passed_up, *weights_of = lax.optimization_barrier(
        (outgoing(begin, half, wide), first_in, up, *weights_of)
    )
    second_in = exchanged(second_out)
    other_up = turned(passed_up, "role", 1)
    first_out = narrow_rows(where, first_in.reshape(-1, width), up, down)
    second_in, first_out = lax.optimization_barrier((second_in, first_out))
    first_back = exchanged(first_out.reshape(owners, FIRST, width))
    second_out = wide_rows(where, second_in.reshape(-1, 2 * width), up, other_up, down, owners)
    second_out, first_back, q_latent = lax.optimization_barrier((second_out, first_back, q_latent))
    second_back = exchanged(second_out)

    packed = attention_part(q_latent, key_value_cache, cache_lengths)
    size = lax.axis_size("tp")
    heads = q_latent.shape[1] // size
    place = lax.axis_index("tp")
    pieces = [
        lax.dynamic_slice_in_dim(packed, (place + step) % size * heads, heads, 1)
        for step in range(size)
    ]
    pieces = [pieces[0]] + [turned(pieces[step], "tp", step) for step in (2, 1, 3)]
    attn_context = attention_join(pieces)
    first_back = first_back.reshape(-1, width)
    second_back = second_back.reshape(-1, width)
    result = jnp.dot(weights_of[0], first_back, preferred_element_type=jnp.float32)
    result = result + jnp.dot(weights_of[1], second_back, preferred_element_type=jnp.float32)
    moe_output = (result[:rows] + result[rows:]).astype(jnp.bfloat16)
    return (attn_context, moe_output)


def solution(mesh):
    return jax.shard_map(
        shards,
        mesh=mesh,
        in_specs=(
            P(("role", "grp"), None, None),
            P(("role", "grp"), "tp", None),
            P(("role", "grp")),
            P("grp", ("role", "tp")),
            P("grp", None),
            P("grp", None),
            P("grp", ("role", "tp"), None),
            P("grp", None, ("role", "tp")),
        ),
        out_specs=(P(("role", "grp"), "tp", None), P("grp", ("role", "tp"))),
        check_vma=False,
    )
```

```python
import functools

import jax
import jax.numpy as jnp
from jax import lax
from jax.experimental import pallas as pl
from jax.experimental.pallas import tpu as pltpu
from jax.sharding import PartitionSpec as P

KEY_VALUE_LATENT = 512
ROPE = 64
QK_NOPE = 128
EXPERTS = 64
CAP = 24
FIRST = 8
TILE = 256
VMEM = 32 * 1024 * 1024
LANES = 128

NEGATIVE = -1e30


def two_halves(value):
    high = value.astype(jnp.bfloat16)
    low = (value - high.astype(jnp.float32)).astype(jnp.bfloat16)
    return high, low


def attention_part(q_latent, key_value_cache, cache_lengths):
    score_scale = 1.0 / (QK_NOPE + ROPE) ** 0.5
    local_len = key_value_cache.shape[1]
    offset = lax.axis_index("tp") * local_len
    positions = offset + jnp.arange(local_len, dtype=jnp.int32)
    is_valid = positions[None, None, :] < cache_lengths[:, None, None]
    scores = (
        jnp.einsum("rhc,rlc->rhl", q_latent, key_value_cache, preferred_element_type=jnp.float32)
        * score_scale
    )
    scores = jnp.where(is_valid, scores, NEGATIVE)
    shift = jnp.max(scores, axis=-1).astype(jnp.bfloat16)
    exp_terms = jnp.where(
        is_valid, jnp.exp(scores - shift.astype(jnp.float32)[..., None]), 0.0
    )
    row_total = jnp.sum(exp_terms, axis=-1)
    context_total = jnp.einsum(
        "wzj,wjp->wzp",
        exp_terms.astype(jnp.bfloat16),
        key_value_cache[:, :, :KEY_VALUE_LATENT],
        preferred_element_type=jnp.float32,
    )
    total_high, total_low = two_halves(row_total)
    stats = jnp.stack([shift, total_high, total_low], axis=-1)
    stats = jnp.pad(stats, ((0, 0), (0, 0), (0, LANES - stats.shape[-1])))
    return jnp.concatenate([context_total.astype(jnp.bfloat16), stats], axis=-1)


def attention_join(pieces):
    mine = jnp.stack(pieces)
    context = mine[..., :KEY_VALUE_LATENT].astype(jnp.float32)
    stats = mine[..., KEY_VALUE_LATENT : KEY_VALUE_LATENT + 3].astype(jnp.float32)
    shift = stats[..., 0]
    total = stats[..., 1] + stats[..., 2]
    factor = jnp.exp(shift - jnp.max(shift, axis=0, keepdims=True))
    total_all = jnp.sum(total * factor, axis=0)
    context_all = jnp.sum(context * factor[..., None], axis=0)
    return (context_all / total_all[..., None]).astype(jnp.bfloat16)


def turned(value, axis, step):
    size = lax.axis_size(axis)
    return lax.ppermute(value, axis, [(k, (k + step) % size) for k in range(size)])


def cost(rows, depth, columns):
    return pl.CostEstimate(
        flops=2 * rows * depth * columns,
        bytes_accessed=2 * (rows * depth + depth * columns + rows * columns),
        transcendentals=0,
    )


def select_kernel(ids_ref, rows_ref, rank_ref, out_ref):
    top, rows = ids_ref.shape
    experts, slots, columns = out_ref.shape
    named = jnp.zeros((experts, rows), jnp.float32)
    numbers = lax.broadcasted_iota(jnp.int32, (experts, rows), 0)
    for k in range(top):
        named = jnp.where(ids_ref[k : k + 1, :] == numbers, 1.0, named)
    above = lax.broadcasted_iota(jnp.int32, (rows, rows), 0)
    right = lax.broadcasted_iota(jnp.int32, (rows, rows), 1)
    before = jnp.dot(
        named.astype(jnp.bfloat16),
        jnp.where(above < right, 1.0, 0.0).astype(jnp.bfloat16),
        preferred_element_type=jnp.float32,
    )
    rank = jnp.where(named > 0.5, before, -1.0)
    rank_ref[...] = rank
    slot = lax.broadcasted_iota(jnp.int32, (experts, slots, rows), 1).astype(jnp.float32)
    placed = jnp.where(rank[:, None, :] == slot, 1.0, 0.0).reshape(experts * slots, rows)
    made = jnp.dot(
        placed.astype(jnp.bfloat16), rows_ref[...], preferred_element_type=jnp.float32
    )
    out_ref[...] = made.reshape(experts, slots, columns).astype(out_ref.dtype)


def first_selection(ids, rows_in):
    rows, columns = rows_in.shape
    return pl.pallas_call(
        select_kernel,
        out_shape=[
            jax.ShapeDtypeStruct((EXPERTS, rows), jnp.float32),
            jax.ShapeDtypeStruct((EXPERTS, FIRST, columns), jnp.bfloat16),
        ],
        compiler_params=pltpu.CompilerParams(vmem_limit_bytes=VMEM),
        cost_estimate=cost(EXPERTS * FIRST, rows, columns),
        name="first_selection",
    )(ids.T, rows_in)


def their_kernel(where, rows_ref, weight_ref, out_ref):
    out_ref[...] = jnp.dot(
        rows_ref[...], weight_ref[...], preferred_element_type=jnp.float32
    ).astype(out_ref.dtype)


def their_half(where, rows_in, weight):
    half, depth = rows_in.shape[0] // 2, rows_in.shape[1]
    columns = weight.shape[2]
    return pl.pallas_call(
        their_kernel,
        out_shape=jax.ShapeDtypeStruct((half, columns), jnp.bfloat16),
        grid_spec=pltpu.PrefetchScalarGridSpec(
            num_scalar_prefetch=1,
            grid=(columns // TILE,),
            in_specs=[
                pl.BlockSpec((half, depth), lambda j, where: (1 - where[0], 0)),
                pl.BlockSpec((None, depth, TILE), lambda j, where: (0, 0, j)),
            ],
            out_specs=pl.BlockSpec((half, TILE), lambda j, where: (0, j)),
        ),
        compiler_params=pltpu.CompilerParams(vmem_limit_bytes=VMEM),
        cost_estimate=cost(half, depth, columns),
        name="their_half",
    )(where, rows_in, weight)


def own_kernel(where, rows_ref, weight_ref, arrived_ref, own_ref, rounded_ref):
    total = jnp.dot(
        rows_ref[...], weight_ref[...], preferred_element_type=jnp.float32
    ) + arrived_ref[...].astype(jnp.float32)
    own_ref[...] = total
    rounded_ref[...] = total.astype(rounded_ref.dtype)


def own_half(where, rows_in, weight, arrived):
    half, depth = rows_in.shape[0] // 2, rows_in.shape[1]
    columns = weight.shape[2]
    return pl.pallas_call(
        own_kernel,
        out_shape=[
            jax.ShapeDtypeStruct((half, columns), jnp.float32),
            jax.ShapeDtypeStruct((half, columns), jnp.bfloat16),
        ],
        grid_spec=pltpu.PrefetchScalarGridSpec(
            num_scalar_prefetch=1,
            grid=(columns // TILE,),
            in_specs=[
                pl.BlockSpec((half, depth), lambda j, where: (where[0], 0)),
                pl.BlockSpec((None, depth, TILE), lambda j, where: (0, 0, j)),
                pl.BlockSpec((half, TILE), lambda j, where: (0, j)),
            ],
            out_specs=[pl.BlockSpec((half, TILE), lambda j, where: (0, j))] * 2,
        ),
        compiler_params=pltpu.CompilerParams(vmem_limit_bytes=VMEM),
        cost_estimate=cost(half, depth, columns),
        name="own_half",
    )(where, rows_in, weight, arrived)


def down_kernel(where, mine_ref, theirs_ref, weight_ref, out_ref):
    @pl.when(pl.program_id(0) == 0)
    def _():
        out_ref[...] = jnp.dot(
            mine_ref[...], weight_ref[...], preferred_element_type=jnp.float32
        ).astype(out_ref.dtype)

    @pl.when(pl.program_id(0) == 1)
    def _():
        out_ref[...] = jnp.dot(
            theirs_ref[...], weight_ref[...], preferred_element_type=jnp.float32
        ).astype(out_ref.dtype)


def down_both(where, mine, theirs, weight):
    half, depth = mine.shape
    columns = weight.shape[2]
    return pl.pallas_call(
        down_kernel,
        out_shape=jax.ShapeDtypeStruct((2 * half, columns), jnp.bfloat16),
        grid_spec=pltpu.PrefetchScalarGridSpec(
            num_scalar_prefetch=1,
            grid=(2,),
            in_specs=[
                pl.BlockSpec((half, depth), lambda h, where: (0, 0)),
                pl.BlockSpec((half, depth), lambda h, where: (0, 0)),
                pl.BlockSpec((None, depth, columns), lambda h, where: (0, 0, 0)),
            ],
            out_specs=pl.BlockSpec(
                (half, columns), lambda h, where: (where[0] + h - 2 * where[0] * h, 0)
            ),
        ),
        compiler_params=pltpu.CompilerParams(vmem_limit_bytes=VMEM),
        cost_estimate=cost(2 * half, depth, columns),
        name="down_both",
    )(where, mine, theirs, weight)


def wide_kernel(where, rows_ref, weight_ref, other_ref, own_ref, *rest):
    piece_refs, total = rest[:-1], rest[-1]
    depth = weight_ref.shape[0]
    share = own_ref.shape[0]
    size = total.shape[0] // share
    total[...] = jnp.dot(
        rows_ref[:, :depth], weight_ref[...], preferred_element_type=jnp.float32
    ) + jnp.dot(rows_ref[:, depth:], other_ref[...], preferred_element_type=jnp.float32)
    for ahead in range(size):
        place = lax.rem(where[1] + ahead, size)
        piece = total[pl.ds(pl.multiple_of(place * share, share), share), :]
        if ahead == 0:
            own_ref[...] = piece
        else:
            piece_refs[ahead - 1][...] = piece.astype(jnp.bfloat16)


def wide_product(where, rows_in, weight, other, size):
    rows, width = rows_in.shape
    _, depth, columns = weight.shape
    share = rows // size
    return pl.pallas_call(
        wide_kernel,
        out_shape=[jax.ShapeDtypeStruct((share, columns), jnp.float32)]
        + [jax.ShapeDtypeStruct((share, columns), jnp.bfloat16)] * (size - 1),
        grid_spec=pltpu.PrefetchScalarGridSpec(
            num_scalar_prefetch=1,
            grid=(columns // TILE,),
            in_specs=[
                pl.BlockSpec((rows, width), lambda j, where: (0, 0)),
                pl.BlockSpec((None, depth, TILE), lambda j, where: (0, 0, j)),
                pl.BlockSpec((None, depth, TILE), lambda j, where: (0, 0, j)),
            ],
            out_specs=[pl.BlockSpec((share, TILE), lambda j, where: (0, j))] * size,
            scratch_shapes=[pltpu.VMEM((rows, TILE), jnp.float32)],
        ),
        compiler_params=pltpu.CompilerParams(vmem_limit_bytes=VMEM),
        cost_estimate=cost(rows, width, columns),
        name="wide_product",
    )(where, rows_in, weight, other)


def down_half_kernel(where, rows_ref, weight_ref, *rest):
    out_ref = rest[-1]
    sources, _, slots, columns = out_ref.shape
    size = 4
    share = sources // size
    together = rows_ref.shape[0] // (share * slots)
    made = jnp.dot(rows_ref[...], weight_ref[...], preferred_element_type=jnp.float32)
    for k in range(together):
        back = pl.program_id(0) * together + k
        place = lax.rem(where[1] + size - back, size)
        piece = made[k * share * slots : (k + 1) * share * slots]
        out_ref[pl.ds(place * share, share), 0] = piece.reshape(share, slots, columns).astype(
            out_ref.dtype
        )


def down_half(where, core, rows_in, weight, made, sources):
    rows, depth = rows_in.shape
    columns = weight.shape[2]
    slots = rows // sources
    tile = rows // 2
    in_specs = [
        pl.BlockSpec((tile, depth), lambda i, where: (i, 0)),
        pl.BlockSpec((None, depth, columns), lambda i, where: (0, 0, 0)),
    ]
    inputs = [rows_in, weight]
    aliases = {}
    if made is not None:
        in_specs.append(pl.BlockSpec(memory_space=pl.ANY))
        inputs.append(made)
        aliases = {3: 0}

    def half(i, where):
        return 0, where[0] + core - 2 * where[0] * core, 0, 0

    return pl.pallas_call(
        down_half_kernel,
        out_shape=jax.ShapeDtypeStruct((sources, 2, slots, columns), jnp.bfloat16),
        grid_spec=pltpu.PrefetchScalarGridSpec(
            num_scalar_prefetch=1,
            grid=(rows // tile,),
            in_specs=in_specs,
            out_specs=pl.BlockSpec((sources, 1, slots, columns), half),
        ),
        input_output_aliases=aliases,
        compiler_params=pltpu.CompilerParams(vmem_limit_bytes=VMEM),
        cost_estimate=cost(rows, depth, columns),
        name="down_half",
    )(where, *inputs)


def narrow_rows(where, rows_in, up, down):
    arrived = turned(their_half(where, rows_in, up), "role", 1)
    own, rounded = own_half(where, rows_in, up, arrived)
    pieces = [turned(rounded, "tp", step) for step in (2, 1, 3)]
    for piece in pieces:
        own = own + piece.astype(jnp.float32)
    mine = jax.nn.silu(own).astype(jnp.bfloat16)
    return down_both(where, mine, turned(mine, "role", 1), down)


def wide_rows(where, rows_in, up, other_up, down, sources):
    size = lax.axis_size("tp")
    own, *pieces = wide_product(where, rows_in, up, other_up, size)
    for step in (2, 1, 3):
        own = own + turned(pieces[step - 1], "tp", step).astype(jnp.float32)
    mine = jax.nn.silu(own).astype(jnp.bfloat16)
    others = {step: turned(mine, "tp", step) for step in (2, 1, 3)}
    mine = jnp.concatenate([mine] + [others[step] for step in range(1, size)], axis=0)
    theirs = turned(mine, "role", 1)
    made = down_half(where, 0, mine, down, None, sources)
    return down_half(where, 1, theirs, down, made, sources)


def shards(
    q_latent,
    key_value_cache,
    cache_lengths,
    hidden,
    expert_ids,
    route_logits,
    up_weight,
    down_weight,
):
    rows, width = hidden.shape
    owners = lax.axis_size("grp")
    experts = jnp.arange(EXPERTS, dtype=jnp.int32)
    where = jnp.stack([lax.axis_index("role"), lax.axis_index("tp")]).astype(jnp.int32)

    rank, first_out = first_selection(expert_ids, hidden)

    def exchanged(value):
        return lax.all_to_all(value, "grp", split_axis=0, concat_axis=0, tiled=True)

    def outgoing(first, count, source):
        slots = (first + jnp.arange(count, dtype=jnp.int32)).astype(jnp.float32)
        placed = rank[:, None, :] == slots[None, :, None]
        placed = placed.reshape(-1, rows).astype(jnp.bfloat16)
        made = jnp.dot(placed, source, preferred_element_type=jnp.float32).astype(jnp.bfloat16)
        return made.reshape(owners, count, source.shape[1])

    def weights(first, last):
        slots = jnp.arange(first, last, dtype=jnp.int32).astype(jnp.float32)
        taken = rank.T[:, :, None] == slots[None, None, :]
        return jnp.where(taken, weight_of[:, :, None], 0.0).reshape(rows, -1).astype(jnp.bfloat16)

    first_out, hidden = lax.optimization_barrier((first_out, hidden))
    first_in = exchanged(first_out)

    wide = jnp.concatenate([hidden, turned(hidden, "role", 1)], axis=1)

    sigmoid_terms = jax.nn.sigmoid(route_logits)
    route_weights = 2.5 * sigmoid_terms / jnp.sum(sigmoid_terms, axis=-1, keepdims=True)
    named = expert_ids[:, None, :] == experts[None, :, None]
    weight_of = jnp.sum(jnp.where(named, route_weights[:, None, :], 0.0), axis=2)
    weights_of = [weights(0, FIRST), weights(FIRST, CAP)]

    half = (CAP - FIRST) // 2
    begin = FIRST + where[0] * half
    second_out, first_in, passed_up, *weights_of = lax.optimization_barrier(
        (outgoing(begin, half, wide), first_in, up_weight, *weights_of)
    )
    second_in = exchanged(second_out)
    other_up = turned(passed_up, "role", 1)
    first_out = narrow_rows(where, first_in.reshape(-1, width), up_weight, down_weight)
    second_in, first_out = lax.optimization_barrier((second_in, first_out))
    first_back = exchanged(first_out.reshape(owners, FIRST, width))
    second_out = wide_rows(where, second_in.reshape(-1, 2 * width), up_weight, other_up, down_weight, owners)
    second_out, first_back, q_latent = lax.optimization_barrier((second_out, first_back, q_latent))
    second_back = exchanged(second_out)

    packed = attention_part(q_latent, key_value_cache, cache_lengths)
    size = lax.axis_size("tp")
    heads = q_latent.shape[1] // size
    place = lax.axis_index("tp")
    pieces = [
        lax.dynamic_slice_in_dim(packed, (place + step) % size * heads, heads, 1)
        for step in range(size)
    ]
    pieces = [pieces[0]] + [turned(pieces[step], "tp", step) for step in (2, 1, 3)]
    attn_context = attention_join(pieces)
    first_back = first_back.reshape(-1, width)
    second_back = second_back.reshape(-1, width)
    result = jnp.dot(weights_of[0], first_back, preferred_element_type=jnp.float32)
    result = result + jnp.dot(weights_of[1], second_back, preferred_element_type=jnp.float32)
    return (attn_context, result.astype(jnp.bfloat16))


def solution(mesh):
    return jax.shard_map(
        shards,
        mesh=mesh,
        in_specs=(
            P(("role", "grp"), None, None),
            P(("role", "grp"), "tp", None),
            P(("role", "grp")),
            P("grp", ("role", "tp")),
            P("grp", None),
            P("grp", None),
            P("grp", ("role", "tp"), None),
            P("grp", None, ("role", "tp")),
        ),
        out_specs=(P(("role", "grp"), "tp", None), P("grp", ("role", "tp"))),
        check_vma=False,
    )
```

```python
import functools

import jax
import jax.numpy as jnp
from jax import lax
from jax.experimental import pallas as pl
from jax.experimental.pallas import tpu as pltpu
from jax.sharding import PartitionSpec as P

KEY_VALUE_LATENT = 512
ROPE = 64
QK_NOPE = 128
EXPERTS = 64
CAP = 24
FIRST = 8
VMEM = 32 * 1024 * 1024
LANES = 128

NEGATIVE = -1e30


def two_halves(value):
    high = value.astype(jnp.bfloat16)
    low = (value - high.astype(jnp.float32)).astype(jnp.bfloat16)
    return high, low


def attention_part(q_latent, key_value_cache, cache_lengths):
    score_scale = 1.0 / (QK_NOPE + ROPE) ** 0.5
    local_len = key_value_cache.shape[1]
    offset = lax.axis_index("tp") * local_len
    positions = offset + jnp.arange(local_len, dtype=jnp.int32)
    is_valid = positions[None, None, :] < cache_lengths[:, None, None]
    scores = (
        jnp.einsum("rhc,rlc->rhl", q_latent, key_value_cache, preferred_element_type=jnp.float32)
        * score_scale
    )
    scores = jnp.where(is_valid, scores, NEGATIVE)
    shift = jnp.max(scores, axis=-1).astype(jnp.bfloat16)
    exp_terms = jnp.where(
        is_valid, jnp.exp(scores - shift.astype(jnp.float32)[..., None]), 0.0
    )
    row_total = jnp.sum(exp_terms, axis=-1)
    context_total = jnp.einsum(
        "wzj,wjp->wzp",
        exp_terms.astype(jnp.bfloat16),
        key_value_cache[:, :, :KEY_VALUE_LATENT],
        preferred_element_type=jnp.float32,
    )
    total_high, total_low = two_halves(row_total)
    stats = jnp.stack([shift, total_high, total_low], axis=-1)
    stats = jnp.pad(stats, ((0, 0), (0, 0), (0, LANES - stats.shape[-1])))
    return jnp.concatenate([context_total.astype(jnp.bfloat16), stats], axis=-1)


def attention_join(pieces):
    mine = jnp.stack(pieces)
    context = mine[..., :KEY_VALUE_LATENT].astype(jnp.float32)
    stats = mine[..., KEY_VALUE_LATENT : KEY_VALUE_LATENT + 3].astype(jnp.float32)
    shift = stats[..., 0]
    total = stats[..., 1] + stats[..., 2]
    factor = jnp.exp(shift - jnp.max(shift, axis=0, keepdims=True))
    total_all = jnp.sum(total * factor, axis=0)
    context_all = jnp.sum(context * factor[..., None], axis=0)
    return (context_all / total_all[..., None]).astype(jnp.bfloat16)


def turned(value, axis, step):
    size = lax.axis_size(axis)
    return lax.ppermute(value, axis, [(k, (k + step) % size) for k in range(size)])


def cost(rows, depth, columns):
    return pl.CostEstimate(
        flops=2 * rows * depth * columns,
        bytes_accessed=2 * (rows * depth + depth * columns + rows * columns),
        transcendentals=0,
    )


def select_kernel(ids_ref, rows_ref, rank_ref, out_ref):
    top, rows = ids_ref.shape
    experts, slots, columns = out_ref.shape
    named = jnp.zeros((experts, rows), jnp.float32)
    numbers = lax.broadcasted_iota(jnp.int32, (experts, rows), 0)
    for k in range(top):
        named = jnp.where(ids_ref[k : k + 1, :] == numbers, 1.0, named)
    above = lax.broadcasted_iota(jnp.int32, (rows, rows), 0)
    right = lax.broadcasted_iota(jnp.int32, (rows, rows), 1)
    before = jnp.dot(
        named.astype(jnp.bfloat16),
        jnp.where(above < right, 1.0, 0.0).astype(jnp.bfloat16),
        preferred_element_type=jnp.float32,
    )
    rank = jnp.where(named > 0.5, before, -1.0)
    rank_ref[...] = rank
    slot = lax.broadcasted_iota(jnp.int32, (experts, slots, rows), 1).astype(jnp.float32)
    placed = jnp.where(rank[:, None, :] == slot, 1.0, 0.0).reshape(experts * slots, rows)
    made = jnp.dot(
        placed.astype(jnp.bfloat16), rows_ref[...], preferred_element_type=jnp.float32
    )
    out_ref[...] = made.reshape(experts, slots, columns).astype(out_ref.dtype)


def first_selection(ids, rows_in):
    rows, columns = rows_in.shape
    return pl.pallas_call(
        select_kernel,
        out_shape=[
            jax.ShapeDtypeStruct((EXPERTS, rows), jnp.float32),
            jax.ShapeDtypeStruct((EXPERTS, FIRST, columns), jnp.bfloat16),
        ],
        compiler_params=pltpu.CompilerParams(vmem_limit_bytes=VMEM),
        cost_estimate=cost(EXPERTS * FIRST, rows, columns),
        name="first_selection",
    )(ids.T, rows_in)


def their_kernel(where, rows_ref, weight_ref, out_ref):
    out_ref[...] = jnp.dot(
        rows_ref[...], weight_ref[...], preferred_element_type=jnp.float32
    ).astype(out_ref.dtype)


def their_half(where, rows_in, weight):
    half, depth = rows_in.shape[0] // 2, rows_in.shape[1]
    columns = weight.shape[1]
    tile = min(256, half)
    steps = half // tile
    return pl.pallas_call(
        their_kernel,
        out_shape=jax.ShapeDtypeStruct((half, columns), jnp.bfloat16),
        grid_spec=pltpu.PrefetchScalarGridSpec(
            num_scalar_prefetch=1,
            grid=(steps,),
            in_specs=[
                pl.BlockSpec((tile, depth), lambda i, where: ((1 - where[0]) * steps + i, 0)),
                pl.BlockSpec((depth, columns), lambda i, where: (0, 0)),
            ],
            out_specs=pl.BlockSpec((tile, columns), lambda i, where: (i, 0)),
        ),
        compiler_params=pltpu.CompilerParams(vmem_limit_bytes=VMEM),
        cost_estimate=cost(half, depth, columns),
        name="their_half",
    )(where, rows_in, weight)


def own_kernel(where, rows_ref, weight_ref, arrived_ref, own_ref, *rest):
    piece_refs, total = rest[:-1], rest[-1]
    tile = rows_ref.shape[0]
    share = own_ref.shape[0]
    size = total.shape[0] // share
    step = pl.program_id(0)
    here = pl.ds(pl.multiple_of(step * tile, tile), tile)
    total[here, :] = jnp.dot(
        rows_ref[...], weight_ref[...], preferred_element_type=jnp.float32
    ) + arrived_ref[...].astype(jnp.float32)

    @pl.when(step == pl.num_programs(0) - 1)
    def _():
        if size == 1:
            own_ref[...] = total[...]
            piece_refs[0][...] = total[...].astype(jnp.bfloat16)
        else:
            for ahead in range(size):
                place = lax.rem(where[1] + ahead, size)
                piece = total[pl.ds(pl.multiple_of(place * share, share), share), :]
                if ahead == 0:
                    own_ref[...] = piece
                else:
                    piece_refs[ahead - 1][...] = piece.astype(jnp.bfloat16)


def own_half(where, rows_in, weight, arrived, size):
    half, depth = rows_in.shape[0] // 2, rows_in.shape[1]
    columns = weight.shape[1]
    tile = min(256, half)
    steps = half // tile
    share = half // size
    return pl.pallas_call(
        own_kernel,
        out_shape=[jax.ShapeDtypeStruct((share, columns), jnp.float32)]
        + [jax.ShapeDtypeStruct((share, columns), jnp.bfloat16)] * max(1, size - 1),
        grid_spec=pltpu.PrefetchScalarGridSpec(
            num_scalar_prefetch=1,
            grid=(steps,),
            in_specs=[
                pl.BlockSpec((tile, depth), lambda i, where: (where[0] * steps + i, 0)),
                pl.BlockSpec((depth, columns), lambda i, where: (0, 0)),
                pl.BlockSpec((tile, columns), lambda i, where: (i, 0)),
            ],
            out_specs=[pl.BlockSpec((share, columns), lambda i, where: (0, 0))]
            * max(2, size),
            scratch_shapes=[pltpu.VMEM((half, columns), jnp.float32)],
        ),
        compiler_params=pltpu.CompilerParams(vmem_limit_bytes=VMEM),
        cost_estimate=cost(half, depth, columns),
        name="own_half",
    )(where, rows_in, weight, arrived)


def copy_kernel(from_ref, to_ref, sem):
    copy = pltpu.make_async_copy(from_ref, to_ref, sem)
    copy.start()
    copy.wait()


def copied(value):
    return pl.pallas_call(
        copy_kernel,
        out_shape=jax.ShapeDtypeStruct(value.shape, value.dtype),
        in_specs=[pl.BlockSpec(memory_space=pl.ANY)],
        out_specs=pl.BlockSpec(memory_space=pl.ANY),
        scratch_shapes=[pltpu.SemaphoreType.DMA],
        name="copied",
    )(value)


def down_kernel(where, mine_ref, theirs_ref, weight_ref, out_ref):
    @pl.when(pl.program_id(0) == 0)
    def _():
        out_ref[...] = jnp.dot(
            mine_ref[...], weight_ref[...], preferred_element_type=jnp.float32
        ).astype(out_ref.dtype)

    @pl.when(pl.program_id(0) == 1)
    def _():
        out_ref[...] = jnp.dot(
            theirs_ref[...], weight_ref[...], preferred_element_type=jnp.float32
        ).astype(out_ref.dtype)


def down_both(where, mine, theirs, weight):
    half, depth = mine.shape
    columns = weight.shape[2]
    return pl.pallas_call(
        down_kernel,
        out_shape=jax.ShapeDtypeStruct((2 * half, columns), jnp.bfloat16),
        grid_spec=pltpu.PrefetchScalarGridSpec(
            num_scalar_prefetch=1,
            grid=(2,),
            in_specs=[
                pl.BlockSpec((half, depth), lambda h, where: (0, 0)),
                pl.BlockSpec((half, depth), lambda h, where: (0, 0)),
                pl.BlockSpec((None, depth, columns), lambda h, where: (0, 0, 0)),
            ],
            out_specs=pl.BlockSpec(
                (half, columns), lambda h, where: (where[0] + h - 2 * where[0] * h, 0)
            ),
        ),
        compiler_params=pltpu.CompilerParams(vmem_limit_bytes=VMEM),
        cost_estimate=cost(2 * half, depth, columns),
        name="down_both",
    )(where, mine, theirs, weight)


def wide_kernel(where, rows_ref, weight_ref, other_ref, own_ref, *rest):
    piece_refs, total = rest[:-1], rest[-1]
    tile = rows_ref.shape[0]
    depth = weight_ref.shape[0]
    share = own_ref.shape[0]
    size = total.shape[0] // share
    step = pl.program_id(0)
    here = pl.ds(pl.multiple_of(step * tile, tile), tile)
    total[here, :] = jnp.dot(
        rows_ref[:, :depth], weight_ref[...], preferred_element_type=jnp.float32
    ) + jnp.dot(rows_ref[:, depth:], other_ref[...], preferred_element_type=jnp.float32)

    @pl.when(step == pl.num_programs(0) - 1)
    def _():
        for ahead in range(size):
            place = lax.rem(where[1] + ahead, size)
            piece = total[pl.ds(pl.multiple_of(place * share, share), share), :]
            if ahead == 0:
                own_ref[...] = piece
            else:
                piece_refs[ahead - 1][...] = piece.astype(jnp.bfloat16)


def wide_product(where, rows_in, weight, other, size):
    rows, width = rows_in.shape
    depth, columns = weight.shape
    tile = 256
    share = rows // size
    return pl.pallas_call(
        wide_kernel,
        out_shape=[jax.ShapeDtypeStruct((share, columns), jnp.float32)]
        + [jax.ShapeDtypeStruct((share, columns), jnp.bfloat16)] * (size - 1),
        grid_spec=pltpu.PrefetchScalarGridSpec(
            num_scalar_prefetch=1,
            grid=(rows // tile,),
            in_specs=[
                pl.BlockSpec((tile, width), lambda i, where: (i, 0)),
                pl.BlockSpec((depth, columns), lambda i, where: (0, 0)),
                pl.BlockSpec((depth, columns), lambda i, where: (0, 0)),
            ],
            out_specs=[pl.BlockSpec((share, columns), lambda i, where: (0, 0))] * size,
            scratch_shapes=[pltpu.VMEM((rows, columns), jnp.float32)],
        ),
        compiler_params=pltpu.CompilerParams(vmem_limit_bytes=VMEM),
        cost_estimate=cost(rows, width, columns),
        name="wide_product",
    )(where, rows_in, weight, other)


def down_half_kernel(where, rows_ref, weight_ref, *rest):
    out_ref = rest[-1]
    sources, _, slots, columns = out_ref.shape
    size = 4
    share = sources // size
    together = rows_ref.shape[0] // (share * slots)
    made = jnp.dot(rows_ref[...], weight_ref[...], preferred_element_type=jnp.float32)
    for k in range(together):
        back = pl.program_id(0) * together + k
        place = lax.rem(where[1] + size - back, size)
        piece = made[k * share * slots : (k + 1) * share * slots]
        out_ref[pl.ds(place * share, share), 0] = piece.reshape(share, slots, columns).astype(
            out_ref.dtype
        )


def down_half(where, core, rows_in, weight, made, sources):
    rows, depth = rows_in.shape
    columns = weight.shape[2]
    slots = rows // sources
    tile = rows // 2
    in_specs = [
        pl.BlockSpec((tile, depth), lambda i, where: (i, 0)),
        pl.BlockSpec((None, depth, columns), lambda i, where: (0, 0, 0)),
    ]
    inputs = [rows_in, weight]
    aliases = {}
    if made is not None:
        in_specs.append(pl.BlockSpec(memory_space=pl.ANY))
        inputs.append(made)
        aliases = {3: 0}

    def half(i, where):
        return 0, where[0] + core - 2 * where[0] * core, 0, 0

    return pl.pallas_call(
        down_half_kernel,
        out_shape=jax.ShapeDtypeStruct((sources, 2, slots, columns), jnp.bfloat16),
        grid_spec=pltpu.PrefetchScalarGridSpec(
            num_scalar_prefetch=1,
            grid=(rows // tile,),
            in_specs=in_specs,
            out_specs=pl.BlockSpec((sources, 1, slots, columns), half),
        ),
        input_output_aliases=aliases,
        compiler_params=pltpu.CompilerParams(vmem_limit_bytes=VMEM),
        cost_estimate=cost(rows, depth, columns),
        name="down_half",
    )(where, *inputs)


def narrow_rows(where, rows_in, up, down):
    arrived = turned(their_half(where, rows_in, up), "role", 1)
    own, rounded = own_half(where, rows_in, up, arrived, 1)
    pieces = [turned(rounded, "tp", step) for step in (2, 1, 3)]
    for piece in pieces:
        own = own + piece.astype(jnp.float32)
    mine = jax.nn.silu(own).astype(jnp.bfloat16)
    return down_both(where, mine, turned(mine, "role", 1), down)


def wide_rows(where, rows_in, up, other_up, down, sources):
    size = lax.axis_size("tp")
    own, *pieces = wide_product(where, rows_in, up, other_up, size)
    for step in (2, 1, 3):
        own = own + turned(pieces[step - 1], "tp", step).astype(jnp.float32)
    mine = jax.nn.silu(own).astype(jnp.bfloat16)
    others = {step: turned(mine, "tp", step) for step in (2, 1, 3)}
    mine = jnp.concatenate([mine] + [others[step] for step in range(1, size)], axis=0)
    theirs = turned(mine, "role", 1)
    made = down_half(where, 0, mine, down, None, sources)
    return down_half(where, 1, theirs, down, made, sources)


def shards(
    q_latent,
    key_value_cache,
    cache_lengths,
    hidden,
    expert_ids,
    route_logits,
    up_weight,
    down_weight,
):
    rows, width = hidden.shape
    owners = lax.axis_size("grp")
    experts = jnp.arange(EXPERTS, dtype=jnp.int32)
    where = jnp.stack([lax.axis_index("role"), lax.axis_index("tp")]).astype(jnp.int32)

    rank, first_out = first_selection(expert_ids, hidden)

    def exchanged(value):
        return lax.all_to_all(value, "grp", split_axis=0, concat_axis=0, tiled=True)

    def outgoing(first, count, source):
        slots = (first + jnp.arange(count, dtype=jnp.int32)).astype(jnp.float32)
        placed = rank[:, None, :] == slots[None, :, None]
        placed = placed.reshape(-1, rows).astype(jnp.bfloat16)
        made = jnp.dot(placed, source, preferred_element_type=jnp.float32).astype(jnp.bfloat16)
        return made.reshape(owners, count, source.shape[1])

    def weights(first, last):
        slots = jnp.arange(first, last, dtype=jnp.int32).astype(jnp.float32)
        taken = rank.T[:, :, None] == slots[None, None, :]
        return jnp.where(taken, weight_of[:, :, None], 0.0).reshape(rows, -1).astype(jnp.bfloat16)

    first_out, hidden = lax.optimization_barrier((first_out, hidden))
    first_in = exchanged(first_out)

    wide = jnp.concatenate([hidden, turned(hidden, "role", 1)], axis=1)
    passed_up = copied(up_weight[0])

    sigmoid_terms = jax.nn.sigmoid(route_logits)
    route_weights = 2.5 * sigmoid_terms / jnp.sum(sigmoid_terms, axis=-1, keepdims=True)
    named = expert_ids[:, None, :] == experts[None, :, None]
    weight_of = jnp.sum(jnp.where(named, route_weights[:, None, :], 0.0), axis=2)
    weights_of = [weights(0, FIRST), weights(FIRST, CAP)]

    half = (CAP - FIRST) // 2
    begin = FIRST + where[0] * half
    second_out, first_in, passed_up, *weights_of = lax.optimization_barrier(
        (outgoing(begin, half, wide), first_in, passed_up, *weights_of)
    )
    second_in = exchanged(second_out)
    other_up = turned(passed_up, "role", 1)
    first_out = narrow_rows(where, first_in.reshape(-1, width), up_weight[0], down_weight)
    second_in, first_out = lax.optimization_barrier((second_in, first_out))
    first_back = exchanged(first_out.reshape(owners, FIRST, width))
    second_out = wide_rows(where, second_in.reshape(-1, 2 * width), up_weight[0], other_up, down_weight, owners)
    second_out, first_back, q_latent = lax.optimization_barrier((second_out, first_back, q_latent))
    second_back = exchanged(second_out)

    packed = attention_part(q_latent, key_value_cache, cache_lengths)
    size = lax.axis_size("tp")
    heads = q_latent.shape[1] // size
    place = lax.axis_index("tp")
    pieces = [
        lax.dynamic_slice_in_dim(packed, (place + step) % size * heads, heads, 1)
        for step in range(size)
    ]
    pieces = [pieces[0]] + [turned(pieces[step], "tp", step) for step in (2, 1, 3)]
    attn_context = attention_join(pieces)
    first_back = first_back.reshape(-1, width)
    second_back = second_back.reshape(-1, width)
    result = jnp.dot(weights_of[0], first_back, preferred_element_type=jnp.float32)
    result = result + jnp.dot(weights_of[1], second_back, preferred_element_type=jnp.float32)
    return (attn_context, result.astype(jnp.bfloat16))


def solution(mesh):
    return jax.shard_map(
        shards,
        mesh=mesh,
        in_specs=(
            P(("role", "grp"), None, None),
            P(("role", "grp"), "tp", None),
            P(("role", "grp")),
            P("grp", ("role", "tp")),
            P("grp", None),
            P("grp", None),
            P("grp", ("role", "tp"), None),
            P("grp", None, ("role", "tp")),
        ),
        out_specs=(P(("role", "grp"), "tp", None), P("grp", ("role", "tp"))),
        check_vma=False,
    )
```

```python
import functools

import jax
import jax.numpy as jnp
from jax import lax
from jax.experimental import pallas as pl
from jax.experimental.pallas import tpu as pltpu
from jax.sharding import PartitionSpec as P

KEY_VALUE_LATENT = 512
ROPE = 64
QK_NOPE = 128
EXPERTS = 64
CAP = 24
FIRST = 8
VMEM = 32 * 1024 * 1024
LANES = 128

NEGATIVE = -1e30


def two_halves(value):
    high = value.astype(jnp.bfloat16)
    low = (value - high.astype(jnp.float32)).astype(jnp.bfloat16)
    return high, low


def attention_part(q_latent, key_value_cache, cache_lengths):
    score_scale = 1.0 / (QK_NOPE + ROPE) ** 0.5
    local_len = key_value_cache.shape[1]
    offset = lax.axis_index("tp") * local_len
    positions = offset + jnp.arange(local_len, dtype=jnp.int32)
    is_valid = positions[None, None, :] < cache_lengths[:, None, None]
    scores = (
        jnp.einsum("rhc,rlc->rhl", q_latent, key_value_cache, preferred_element_type=jnp.float32)
        * score_scale
    )
    scores = jnp.where(is_valid, scores, NEGATIVE)
    shift = jnp.max(scores, axis=-1).astype(jnp.bfloat16)
    exp_terms = jnp.where(
        is_valid, jnp.exp(scores - shift.astype(jnp.float32)[..., None]), 0.0
    )
    row_total = jnp.sum(exp_terms, axis=-1)
    context_total = jnp.einsum(
        "wzj,wjp->wzp",
        exp_terms.astype(jnp.bfloat16),
        key_value_cache[:, :, :KEY_VALUE_LATENT],
        preferred_element_type=jnp.float32,
    )
    total_high, total_low = two_halves(row_total)
    stats = jnp.stack([shift, total_high, total_low], axis=-1)
    stats = jnp.pad(stats, ((0, 0), (0, 0), (0, LANES - stats.shape[-1])))
    return jnp.concatenate([context_total.astype(jnp.bfloat16), stats], axis=-1)


def attention_join(pieces):
    mine = jnp.stack(pieces)
    context = mine[..., :KEY_VALUE_LATENT].astype(jnp.float32)
    stats = mine[..., KEY_VALUE_LATENT : KEY_VALUE_LATENT + 3].astype(jnp.float32)
    shift = stats[..., 0]
    total = stats[..., 1] + stats[..., 2]
    factor = jnp.exp(shift - jnp.max(shift, axis=0, keepdims=True))
    total_all = jnp.sum(total * factor, axis=0)
    context_all = jnp.sum(context * factor[..., None], axis=0)
    return (context_all / total_all[..., None]).astype(jnp.bfloat16)


def turned(value, axis, step):
    size = lax.axis_size(axis)
    return lax.ppermute(value, axis, [(k, (k + step) % size) for k in range(size)])


def cost(rows, depth, columns):
    return pl.CostEstimate(
        flops=2 * rows * depth * columns,
        bytes_accessed=2 * (rows * depth + depth * columns + rows * columns),
        transcendentals=0,
    )


def select_kernel(ids_ref, rows_ref, rank_ref, out_ref):
    top, rows = ids_ref.shape
    experts, slots, columns = out_ref.shape
    named = jnp.zeros((experts, rows), jnp.float32)
    numbers = lax.broadcasted_iota(jnp.int32, (experts, rows), 0)
    for k in range(top):
        named = jnp.where(ids_ref[k : k + 1, :] == numbers, 1.0, named)
    above = lax.broadcasted_iota(jnp.int32, (rows, rows), 0)
    right = lax.broadcasted_iota(jnp.int32, (rows, rows), 1)
    before = jnp.dot(
        named.astype(jnp.bfloat16),
        jnp.where(above < right, 1.0, 0.0).astype(jnp.bfloat16),
        preferred_element_type=jnp.float32,
    )
    rank = jnp.where(named > 0.5, before, -1.0)
    rank_ref[...] = rank
    slot = lax.broadcasted_iota(jnp.int32, (experts, slots, rows), 1).astype(jnp.float32)
    placed = jnp.where(rank[:, None, :] == slot, 1.0, 0.0).reshape(experts * slots, rows)
    made = jnp.dot(
        placed.astype(jnp.bfloat16), rows_ref[...], preferred_element_type=jnp.float32
    )
    out_ref[...] = made.reshape(experts, slots, columns).astype(out_ref.dtype)


def first_selection(ids, rows_in):
    rows, columns = rows_in.shape
    return pl.pallas_call(
        select_kernel,
        out_shape=[
            jax.ShapeDtypeStruct((EXPERTS, rows), jnp.float32),
            jax.ShapeDtypeStruct((EXPERTS, FIRST, columns), jnp.bfloat16),
        ],
        compiler_params=pltpu.CompilerParams(vmem_limit_bytes=VMEM),
        cost_estimate=cost(EXPERTS * FIRST, rows, columns),
        name="first_selection",
    )(ids.T, rows_in)


def their_kernel(where, rows_ref, weight_ref, out_ref):
    out_ref[...] = jnp.dot(
        rows_ref[...], weight_ref[...], preferred_element_type=jnp.float32
    ).astype(out_ref.dtype)


def their_half(where, rows_in, weight):
    half, depth = rows_in.shape[0] // 2, rows_in.shape[1]
    columns = weight.shape[1]
    tile = min(256, half)
    steps = half // tile
    return pl.pallas_call(
        their_kernel,
        out_shape=jax.ShapeDtypeStruct((half, columns), jnp.bfloat16),
        grid_spec=pltpu.PrefetchScalarGridSpec(
            num_scalar_prefetch=1,
            grid=(steps,),
            in_specs=[
                pl.BlockSpec((tile, depth), lambda i, where: ((1 - where[0]) * steps + i, 0)),
                pl.BlockSpec((depth, columns), lambda i, where: (0, 0)),
            ],
            out_specs=pl.BlockSpec((tile, columns), lambda i, where: (i, 0)),
        ),
        compiler_params=pltpu.CompilerParams(vmem_limit_bytes=VMEM),
        cost_estimate=cost(half, depth, columns),
        name="their_half",
    )(where, rows_in, weight)


def own_kernel(where, rows_ref, weight_ref, arrived_ref, own_ref, *rest):
    piece_refs, total = rest[:-1], rest[-1]
    tile = rows_ref.shape[0]
    share = own_ref.shape[0]
    size = total.shape[0] // share
    step = pl.program_id(0)
    here = pl.ds(pl.multiple_of(step * tile, tile), tile)
    total[here, :] = jnp.dot(
        rows_ref[...], weight_ref[...], preferred_element_type=jnp.float32
    ) + arrived_ref[...].astype(jnp.float32)

    @pl.when(step == pl.num_programs(0) - 1)
    def _():
        if size == 1:
            own_ref[...] = total[...]
            piece_refs[0][...] = total[...].astype(jnp.bfloat16)
        else:
            for ahead in range(size):
                place = lax.rem(where[1] + ahead, size)
                piece = total[pl.ds(pl.multiple_of(place * share, share), share), :]
                if ahead == 0:
                    own_ref[...] = piece
                else:
                    piece_refs[ahead - 1][...] = piece.astype(jnp.bfloat16)


def own_half(where, rows_in, weight, arrived, size):
    half, depth = rows_in.shape[0] // 2, rows_in.shape[1]
    columns = weight.shape[1]
    tile = min(256, half)
    steps = half // tile
    share = half // size
    return pl.pallas_call(
        own_kernel,
        out_shape=[jax.ShapeDtypeStruct((share, columns), jnp.float32)]
        + [jax.ShapeDtypeStruct((share, columns), jnp.bfloat16)] * max(1, size - 1),
        grid_spec=pltpu.PrefetchScalarGridSpec(
            num_scalar_prefetch=1,
            grid=(steps,),
            in_specs=[
                pl.BlockSpec((tile, depth), lambda i, where: (where[0] * steps + i, 0)),
                pl.BlockSpec((depth, columns), lambda i, where: (0, 0)),
                pl.BlockSpec((tile, columns), lambda i, where: (i, 0)),
            ],
            out_specs=[pl.BlockSpec((share, columns), lambda i, where: (0, 0))]
            * max(2, size),
            scratch_shapes=[pltpu.VMEM((half, columns), jnp.float32)],
        ),
        compiler_params=pltpu.CompilerParams(vmem_limit_bytes=VMEM),
        cost_estimate=cost(half, depth, columns),
        name="own_half",
    )(where, rows_in, weight, arrived)


def copy_kernel(from_ref, to_ref):
    to_ref[...] = from_ref[...]


def copied(value):
    rows, columns = value.shape
    tile = 128
    return pl.pallas_call(
        copy_kernel,
        out_shape=jax.ShapeDtypeStruct(value.shape, value.dtype),
        grid=(rows // tile,),
        in_specs=[pl.BlockSpec((tile, columns), lambda i: (i, 0))],
        out_specs=pl.BlockSpec((tile, columns), lambda i: (i, 0)),
        compiler_params=pltpu.CompilerParams(vmem_limit_bytes=VMEM),
        cost_estimate=pl.CostEstimate(
            flops=0, bytes_accessed=4 * rows * columns, transcendentals=0
        ),
        name="copied",
    )(value)


def down_kernel(where, mine_ref, theirs_ref, weight_ref, out_ref):
    @pl.when(pl.program_id(0) == 0)
    def _():
        out_ref[...] = jnp.dot(
            mine_ref[...], weight_ref[...], preferred_element_type=jnp.float32
        ).astype(out_ref.dtype)

    @pl.when(pl.program_id(0) == 1)
    def _():
        out_ref[...] = jnp.dot(
            theirs_ref[...], weight_ref[...], preferred_element_type=jnp.float32
        ).astype(out_ref.dtype)


def down_both(where, mine, theirs, weight):
    half, depth = mine.shape
    columns = weight.shape[2]
    return pl.pallas_call(
        down_kernel,
        out_shape=jax.ShapeDtypeStruct((2 * half, columns), jnp.bfloat16),
        grid_spec=pltpu.PrefetchScalarGridSpec(
            num_scalar_prefetch=1,
            grid=(2,),
            in_specs=[
                pl.BlockSpec((half, depth), lambda h, where: (0, 0)),
                pl.BlockSpec((half, depth), lambda h, where: (0, 0)),
                pl.BlockSpec((None, depth, columns), lambda h, where: (0, 0, 0)),
            ],
            out_specs=pl.BlockSpec(
                (half, columns), lambda h, where: (where[0] + h - 2 * where[0] * h, 0)
            ),
        ),
        compiler_params=pltpu.CompilerParams(vmem_limit_bytes=VMEM),
        cost_estimate=cost(2 * half, depth, columns),
        name="down_both",
    )(where, mine, theirs, weight)


def wide_kernel(where, rows_ref, weight_ref, other_ref, own_ref, *rest):
    piece_refs, total = rest[:-1], rest[-1]
    tile = rows_ref.shape[0]
    depth = weight_ref.shape[0]
    share = own_ref.shape[0]
    size = total.shape[0] // share
    step = pl.program_id(0)
    here = pl.ds(pl.multiple_of(step * tile, tile), tile)
    total[here, :] = jnp.dot(
        rows_ref[:, :depth], weight_ref[...], preferred_element_type=jnp.float32
    ) + jnp.dot(rows_ref[:, depth:], other_ref[...], preferred_element_type=jnp.float32)

    @pl.when(step == pl.num_programs(0) - 1)
    def _():
        for ahead in range(size):
            place = lax.rem(where[1] + ahead, size)
            piece = total[pl.ds(pl.multiple_of(place * share, share), share), :]
            if ahead == 0:
                own_ref[...] = piece
            else:
                piece_refs[ahead - 1][...] = piece.astype(jnp.bfloat16)


def wide_product(where, rows_in, weight, other, size):
    rows, width = rows_in.shape
    depth, columns = weight.shape
    tile = 256
    share = rows // size
    return pl.pallas_call(
        wide_kernel,
        out_shape=[jax.ShapeDtypeStruct((share, columns), jnp.float32)]
        + [jax.ShapeDtypeStruct((share, columns), jnp.bfloat16)] * (size - 1),
        grid_spec=pltpu.PrefetchScalarGridSpec(
            num_scalar_prefetch=1,
            grid=(rows // tile,),
            in_specs=[
                pl.BlockSpec((tile, width), lambda i, where: (i, 0)),
                pl.BlockSpec((depth, columns), lambda i, where: (0, 0)),
                pl.BlockSpec((depth, columns), lambda i, where: (0, 0)),
            ],
            out_specs=[pl.BlockSpec((share, columns), lambda i, where: (0, 0))] * size,
            scratch_shapes=[pltpu.VMEM((rows, columns), jnp.float32)],
        ),
        compiler_params=pltpu.CompilerParams(vmem_limit_bytes=VMEM),
        cost_estimate=cost(rows, width, columns),
        name="wide_product",
    )(where, rows_in, weight, other)


def down_half_kernel(where, rows_ref, weight_ref, *rest):
    out_ref = rest[-1]
    sources, _, slots, columns = out_ref.shape
    size = 4
    share = sources // size
    together = rows_ref.shape[0] // (share * slots)
    made = jnp.dot(rows_ref[...], weight_ref[...], preferred_element_type=jnp.float32)
    for k in range(together):
        back = pl.program_id(0) * together + k
        step = jnp.where(back < 2, back, 5 - back)
        place = lax.rem(where[1] + size - step, size)
        piece = made[k * share * slots : (k + 1) * share * slots]
        out_ref[pl.ds(place * share, share), 0] = piece.reshape(share, slots, columns).astype(
            out_ref.dtype
        )


def down_half(where, core, rows_in, weight, made, sources):
    rows, depth = rows_in.shape
    columns = weight.shape[2]
    slots = rows // sources
    tile = rows // 2
    in_specs = [
        pl.BlockSpec((tile, depth), lambda i, where: (i, 0)),
        pl.BlockSpec((None, depth, columns), lambda i, where: (0, 0, 0)),
    ]
    inputs = [rows_in, weight]
    aliases = {}
    if made is not None:
        in_specs.append(pl.BlockSpec(memory_space=pl.ANY))
        inputs.append(made)
        aliases = {3: 0}

    def half(i, where):
        return 0, where[0] + core - 2 * where[0] * core, 0, 0

    return pl.pallas_call(
        down_half_kernel,
        out_shape=jax.ShapeDtypeStruct((sources, 2, slots, columns), jnp.bfloat16),
        grid_spec=pltpu.PrefetchScalarGridSpec(
            num_scalar_prefetch=1,
            grid=(rows // tile,),
            in_specs=in_specs,
            out_specs=pl.BlockSpec((sources, 1, slots, columns), half),
        ),
        input_output_aliases=aliases,
        compiler_params=pltpu.CompilerParams(vmem_limit_bytes=VMEM),
        cost_estimate=cost(rows, depth, columns),
        name="down_half",
    )(where, *inputs)


def narrow_rows(where, rows_in, up, down):
    arrived = turned(their_half(where, rows_in, up), "role", 1)
    own, rounded = own_half(where, rows_in, up, arrived, 1)
    pieces = [turned(rounded, "tp", step) for step in (3, 1, 2)]
    for piece in pieces:
        own = own + piece.astype(jnp.float32)
    mine = jax.nn.silu(own).astype(jnp.bfloat16)
    return down_both(where, mine, turned(mine, "role", 1), down)


def wide_rows(where, rows_in, up, other_up, down, sources):
    size = lax.axis_size("tp")
    own, *pieces = wide_product(where, rows_in, up, other_up, size)
    for step in (3, 1, 2):
        own = own + turned(pieces[step - 1], "tp", step).astype(jnp.float32)
    mine = jax.nn.silu(own).astype(jnp.bfloat16)
    others = {step: turned(mine, "tp", step) for step in (3, 1, 2)}
    mine = jnp.concatenate([mine, others[1], others[3], others[2]], axis=0)
    theirs = turned(mine, "role", 1)
    made = down_half(where, 0, mine, down, None, sources)
    return down_half(where, 1, theirs, down, made, sources)


def shards(
    q_latent,
    key_value_cache,
    cache_lengths,
    hidden,
    expert_ids,
    route_logits,
    up_weight,
    down_weight,
):
    rows, width = hidden.shape
    owners = lax.axis_size("grp")
    experts = jnp.arange(EXPERTS, dtype=jnp.int32)
    where = jnp.stack([lax.axis_index("role"), lax.axis_index("tp")]).astype(jnp.int32)

    rank, first_out = first_selection(expert_ids, hidden)

    def exchanged(value):
        return lax.all_to_all(value, "grp", split_axis=0, concat_axis=0, tiled=True)

    def outgoing(first, count, source):
        slots = (first + jnp.arange(count, dtype=jnp.int32)).astype(jnp.float32)
        placed = rank[:, None, :] == slots[None, :, None]
        placed = placed.reshape(-1, rows).astype(jnp.bfloat16)
        made = jnp.dot(placed, source, preferred_element_type=jnp.float32).astype(jnp.bfloat16)
        return made.reshape(owners, count, source.shape[1])

    def weights(first, last):
        slots = jnp.arange(first, last, dtype=jnp.int32).astype(jnp.float32)
        taken = rank.T[:, :, None] == slots[None, None, :]
        return jnp.where(taken, weight_of[:, :, None], 0.0).reshape(rows, -1).astype(jnp.bfloat16)

    first_out, hidden = lax.optimization_barrier((first_out, hidden))
    first_in = exchanged(first_out)

    wide = jnp.concatenate([hidden, turned(hidden, "role", 1)], axis=1)
    passed_up = copied(up_weight[0])

    sigmoid_terms = jax.nn.sigmoid(route_logits)
    route_weights = 2.5 * sigmoid_terms / jnp.sum(sigmoid_terms, axis=-1, keepdims=True)
    named = expert_ids[:, None, :] == experts[None, :, None]
    weight_of = jnp.sum(jnp.where(named, route_weights[:, None, :], 0.0), axis=2)
    weights_of = [weights(0, FIRST), weights(FIRST, CAP)]

    half = (CAP - FIRST) // 2
    begin = FIRST + where[0] * half
    second_out, first_in, passed_up, *weights_of = lax.optimization_barrier(
        (outgoing(begin, half, wide), first_in, passed_up, *weights_of)
    )
    second_in = exchanged(second_out)
    other_up = turned(passed_up, "role", 1)
    first_out = narrow_rows(where, first_in.reshape(-1, width), up_weight[0], down_weight)
    second_in, first_out = lax.optimization_barrier((second_in, first_out))
    first_back = exchanged(first_out.reshape(owners, FIRST, width))
    second_out = wide_rows(where, second_in.reshape(-1, 2 * width), up_weight[0], other_up, down_weight, owners)
    second_out, first_back, q_latent = lax.optimization_barrier((second_out, first_back, q_latent))
    second_back = exchanged(second_out)

    packed = attention_part(q_latent, key_value_cache, cache_lengths)
    size = lax.axis_size("tp")
    heads = q_latent.shape[1] // size
    place = lax.axis_index("tp")
    pieces = [
        lax.dynamic_slice_in_dim(packed, (place + step) % size * heads, heads, 1)
        for step in range(size)
    ]
    pieces = [pieces[0]] + [turned(pieces[step], "tp", step) for step in (2, 1, 3)]
    attn_context = attention_join(pieces)
    first_back = first_back.reshape(-1, width)
    second_back = second_back.reshape(-1, width)
    result = jnp.dot(weights_of[0], first_back, preferred_element_type=jnp.float32)
    result = result + jnp.dot(weights_of[1], second_back, preferred_element_type=jnp.float32)
    return (attn_context, result.astype(jnp.bfloat16))


def solution(mesh):
    return jax.shard_map(
        shards,
        mesh=mesh,
        in_specs=(
            P(("role", "grp"), None, None),
            P(("role", "grp"), "tp", None),
            P(("role", "grp")),
            P("grp", ("role", "tp")),
            P("grp", None),
            P("grp", None),
            P("grp", ("role", "tp"), None),
            P("grp", None, ("role", "tp")),
        ),
        out_specs=(P(("role", "grp"), "tp", None), P("grp", ("role", "tp"))),
        check_vma=False,
    )
```

```python
import functools

import jax
import jax.numpy as jnp
from jax import lax
from jax.experimental import pallas as pl
from jax.experimental.pallas import tpu as pltpu
from jax.sharding import PartitionSpec as P

KEY_VALUE_LATENT = 512
ROPE = 64
QK_NOPE = 128
EXPERTS = 64
CAP = 24
FIRST = 8
VMEM = 32 * 1024 * 1024
MOST = 60 * 1024 * 1024
LANES = 128

NEGATIVE = -1e30


def two_halves(value):
    high = value.astype(jnp.bfloat16)
    low = (value - high.astype(jnp.float32)).astype(jnp.bfloat16)
    return high, low


def attention_part(q_latent, key_value_cache, cache_lengths):
    score_scale = 1.0 / (QK_NOPE + ROPE) ** 0.5
    local_len = key_value_cache.shape[1]
    offset = lax.axis_index("tp") * local_len
    positions = offset + jnp.arange(local_len, dtype=jnp.int32)
    is_valid = positions[None, None, :] < cache_lengths[:, None, None]
    scores = (
        jnp.einsum("rhc,rlc->rhl", q_latent, key_value_cache, preferred_element_type=jnp.float32)
        * score_scale
    )
    scores = jnp.where(is_valid, scores, NEGATIVE)
    shift = jnp.max(scores, axis=-1).astype(jnp.bfloat16)
    exp_terms = jnp.where(
        is_valid, jnp.exp(scores - shift.astype(jnp.float32)[..., None]), 0.0
    )
    row_total = jnp.sum(exp_terms, axis=-1)
    context_total = jnp.einsum(
        "wzj,wjp->wzp",
        exp_terms.astype(jnp.bfloat16),
        key_value_cache[:, :, :KEY_VALUE_LATENT],
        preferred_element_type=jnp.float32,
    )
    total_high, total_low = two_halves(row_total)
    stats = jnp.stack([shift, total_high, total_low], axis=-1)
    stats = jnp.pad(stats, ((0, 0), (0, 0), (0, LANES - stats.shape[-1])))
    return jnp.concatenate([context_total.astype(jnp.bfloat16), stats], axis=-1)


def attention_join(pieces):
    mine = jnp.stack(pieces)
    context = mine[..., :KEY_VALUE_LATENT].astype(jnp.float32)
    stats = mine[..., KEY_VALUE_LATENT : KEY_VALUE_LATENT + 3].astype(jnp.float32)
    shift = stats[..., 0]
    total = stats[..., 1] + stats[..., 2]
    factor = jnp.exp(shift - jnp.max(shift, axis=0, keepdims=True))
    total_all = jnp.sum(total * factor, axis=0)
    context_all = jnp.sum(context * factor[..., None], axis=0)
    return (context_all / total_all[..., None]).astype(jnp.bfloat16)


def turned(value, axis, step):
    size = lax.axis_size(axis)
    return lax.ppermute(value, axis, [(k, (k + step) % size) for k in range(size)])


def cost(rows, depth, columns):
    return pl.CostEstimate(
        flops=2 * rows * depth * columns,
        bytes_accessed=2 * (rows * depth + depth * columns + rows * columns),
        transcendentals=0,
    )


def select_kernel(ids_ref, rows_ref, rank_ref, out_ref):
    top, rows = ids_ref.shape
    experts, slots, columns = out_ref.shape
    named = jnp.zeros((experts, rows), jnp.float32)
    numbers = lax.broadcasted_iota(jnp.int32, (experts, rows), 0)
    for k in range(top):
        named = jnp.where(ids_ref[k : k + 1, :] == numbers, 1.0, named)
    above = lax.broadcasted_iota(jnp.int32, (rows, rows), 0)
    right = lax.broadcasted_iota(jnp.int32, (rows, rows), 1)
    before = jnp.dot(
        named.astype(jnp.bfloat16),
        jnp.where(above < right, 1.0, 0.0).astype(jnp.bfloat16),
        preferred_element_type=jnp.float32,
    )
    rank = jnp.where(named > 0.5, before, -1.0)
    rank_ref[...] = rank
    slot = lax.broadcasted_iota(jnp.int32, (experts, slots, rows), 1).astype(jnp.float32)
    placed = jnp.where(rank[:, None, :] == slot, 1.0, 0.0).reshape(experts * slots, rows)
    made = jnp.dot(
        placed.astype(jnp.bfloat16), rows_ref[...], preferred_element_type=jnp.float32
    )
    out_ref[...] = made.reshape(experts, slots, columns).astype(out_ref.dtype)


def first_selection(ids, rows_in):
    rows, columns = rows_in.shape
    return pl.pallas_call(
        select_kernel,
        out_shape=[
            jax.ShapeDtypeStruct((EXPERTS, rows), jnp.float32),
            jax.ShapeDtypeStruct((EXPERTS, FIRST, columns), jnp.bfloat16),
        ],
        compiler_params=pltpu.CompilerParams(vmem_limit_bytes=MOST),
        cost_estimate=cost(EXPERTS * FIRST, rows, columns),
        name="first_selection",
    )(ids.T, rows_in)


def their_kernel(where, rows_ref, weight_ref, out_ref):
    out_ref[...] = jnp.dot(
        rows_ref[...], weight_ref[...], preferred_element_type=jnp.float32
    ).astype(out_ref.dtype)


def their_half(where, rows_in, weight):
    half, depth = rows_in.shape[0] // 2, rows_in.shape[1]
    columns = weight.shape[1]
    tile = min(256, half)
    steps = half // tile
    return pl.pallas_call(
        their_kernel,
        out_shape=jax.ShapeDtypeStruct((half, columns), jnp.bfloat16),
        grid_spec=pltpu.PrefetchScalarGridSpec(
            num_scalar_prefetch=1,
            grid=(steps,),
            in_specs=[
                pl.BlockSpec((tile, depth), lambda i, where: ((1 - where[0]) * steps + i, 0)),
                pl.BlockSpec((depth, columns), lambda i, where: (0, 0)),
            ],
            out_specs=pl.BlockSpec((tile, columns), lambda i, where: (i, 0)),
        ),
        compiler_params=pltpu.CompilerParams(vmem_limit_bytes=VMEM),
        cost_estimate=cost(half, depth, columns),
        name="their_half",
    )(where, rows_in, weight)


def own_kernel(where, rows_ref, weight_ref, arrived_ref, own_ref, *rest):
    piece_refs, total = rest[:-1], rest[-1]
    tile = rows_ref.shape[0]
    share = own_ref.shape[0]
    size = total.shape[0] // share
    step = pl.program_id(0)
    here = pl.ds(pl.multiple_of(step * tile, tile), tile)
    total[here, :] = jnp.dot(
        rows_ref[...], weight_ref[...], preferred_element_type=jnp.float32
    ) + arrived_ref[...].astype(jnp.float32)

    @pl.when(step == pl.num_programs(0) - 1)
    def _():
        if size == 1:
            own_ref[...] = total[...]
            piece_refs[0][...] = total[...].astype(jnp.bfloat16)
        else:
            for ahead in range(size):
                place = lax.rem(where[1] + ahead, size)
                piece = total[pl.ds(pl.multiple_of(place * share, share), share), :]
                if ahead == 0:
                    own_ref[...] = piece
                else:
                    piece_refs[ahead - 1][...] = piece.astype(jnp.bfloat16)


def own_half(where, rows_in, weight, arrived, size):
    half, depth = rows_in.shape[0] // 2, rows_in.shape[1]
    columns = weight.shape[1]
    tile = min(256, half)
    steps = half // tile
    share = half // size
    return pl.pallas_call(
        own_kernel,
        out_shape=[jax.ShapeDtypeStruct((share, columns), jnp.float32)]
        + [jax.ShapeDtypeStruct((share, columns), jnp.bfloat16)] * max(1, size - 1),
        grid_spec=pltpu.PrefetchScalarGridSpec(
            num_scalar_prefetch=1,
            grid=(steps,),
            in_specs=[
                pl.BlockSpec((tile, depth), lambda i, where: (where[0] * steps + i, 0)),
                pl.BlockSpec((depth, columns), lambda i, where: (0, 0)),
                pl.BlockSpec((tile, columns), lambda i, where: (i, 0)),
            ],
            out_specs=[pl.BlockSpec((share, columns), lambda i, where: (0, 0))]
            * max(2, size),
            scratch_shapes=[pltpu.VMEM((half, columns), jnp.float32)],
        ),
        compiler_params=pltpu.CompilerParams(vmem_limit_bytes=VMEM),
        cost_estimate=cost(half, depth, columns),
        name="own_half",
    )(where, rows_in, weight, arrived)


def combine_kernel(weights_ref, rows_ref, out_ref):
    out_ref[...] = jnp.dot(weights_ref[...], rows_ref[...], preferred_element_type=jnp.float32)


def combined(weights, rows_in):
    rows, depth = weights.shape
    columns = rows_in.shape[1]
    return pl.pallas_call(
        combine_kernel,
        out_shape=jax.ShapeDtypeStruct((rows, columns), jnp.float32),
        compiler_params=pltpu.CompilerParams(vmem_limit_bytes=MOST),
        cost_estimate=cost(rows, depth, columns),
        name="combined",
    )(weights, rows_in)


def copy_kernel(from_ref, to_ref):
    to_ref[...] = from_ref[...]


def copied(value):
    rows, columns = value.shape
    tile = 128
    return pl.pallas_call(
        copy_kernel,
        out_shape=jax.ShapeDtypeStruct(value.shape, value.dtype),
        grid=(rows // tile,),
        in_specs=[pl.BlockSpec((tile, columns), lambda i: (i, 0))],
        out_specs=pl.BlockSpec((tile, columns), lambda i: (i, 0)),
        compiler_params=pltpu.CompilerParams(vmem_limit_bytes=VMEM),
        cost_estimate=pl.CostEstimate(
            flops=0, bytes_accessed=4 * rows * columns, transcendentals=0
        ),
        name="copied",
    )(value)


def down_kernel(where, mine_ref, theirs_ref, weight_ref, out_ref):
    @pl.when(pl.program_id(0) == 0)
    def _():
        out_ref[...] = jnp.dot(
            mine_ref[...], weight_ref[...], preferred_element_type=jnp.float32
        ).astype(out_ref.dtype)

    @pl.when(pl.program_id(0) == 1)
    def _():
        out_ref[...] = jnp.dot(
            theirs_ref[...], weight_ref[...], preferred_element_type=jnp.float32
        ).astype(out_ref.dtype)


def down_both(where, mine, theirs, weight):
    half, depth = mine.shape
    columns = weight.shape[2]
    return pl.pallas_call(
        down_kernel,
        out_shape=jax.ShapeDtypeStruct((2 * half, columns), jnp.bfloat16),
        grid_spec=pltpu.PrefetchScalarGridSpec(
            num_scalar_prefetch=1,
            grid=(2,),
            in_specs=[
                pl.BlockSpec((half, depth), lambda h, where: (0, 0)),
                pl.BlockSpec((half, depth), lambda h, where: (0, 0)),
                pl.BlockSpec((None, depth, columns), lambda h, where: (0, 0, 0)),
            ],
            out_specs=pl.BlockSpec(
                (half, columns), lambda h, where: (where[0] + h - 2 * where[0] * h, 0)
            ),
        ),
        compiler_params=pltpu.CompilerParams(vmem_limit_bytes=VMEM),
        cost_estimate=cost(2 * half, depth, columns),
        name="down_both",
    )(where, mine, theirs, weight)


def wide_kernel(where, rows_ref, weight_ref, other_ref, own_ref, *rest):
    piece_refs, total = rest[:-1], rest[-1]
    tile = rows_ref.shape[0]
    depth = weight_ref.shape[0]
    share = own_ref.shape[0]
    size = total.shape[0] // share
    step = pl.program_id(0)
    here = pl.ds(pl.multiple_of(step * tile, tile), tile)
    total[here, :] = jnp.dot(
        rows_ref[:, :depth], weight_ref[...], preferred_element_type=jnp.float32
    ) + jnp.dot(rows_ref[:, depth:], other_ref[...], preferred_element_type=jnp.float32)

    @pl.when(step == pl.num_programs(0) - 1)
    def _():
        for ahead in range(size):
            place = lax.rem(where[1] + ahead, size)
            piece = total[pl.ds(pl.multiple_of(place * share, share), share), :]
            if ahead == 0:
                own_ref[...] = piece
            else:
                piece_refs[ahead - 1][...] = piece.astype(jnp.bfloat16)


def wide_product(where, rows_in, weight, other, size):
    rows, width = rows_in.shape
    depth, columns = weight.shape
    tile = 256
    share = rows // size
    return pl.pallas_call(
        wide_kernel,
        out_shape=[jax.ShapeDtypeStruct((share, columns), jnp.float32)]
        + [jax.ShapeDtypeStruct((share, columns), jnp.bfloat16)] * (size - 1),
        grid_spec=pltpu.PrefetchScalarGridSpec(
            num_scalar_prefetch=1,
            grid=(rows // tile,),
            in_specs=[
                pl.BlockSpec((tile, width), lambda i, where: (i, 0)),
                pl.BlockSpec((depth, columns), lambda i, where: (0, 0)),
                pl.BlockSpec((depth, columns), lambda i, where: (0, 0)),
            ],
            out_specs=[pl.BlockSpec((share, columns), lambda i, where: (0, 0))] * size,
            scratch_shapes=[pltpu.VMEM((rows, columns), jnp.float32)],
        ),
        compiler_params=pltpu.CompilerParams(vmem_limit_bytes=VMEM),
        cost_estimate=cost(rows, width, columns),
        name="wide_product",
    )(where, rows_in, weight, other)


def down_half_kernel(where, rows_ref, weight_ref, *rest):
    out_ref = rest[-1]
    sources, _, slots, columns = out_ref.shape
    size = 4
    share = sources // size
    together = rows_ref.shape[0] // (share * slots)
    made = jnp.dot(rows_ref[...], weight_ref[...], preferred_element_type=jnp.float32)
    for k in range(together):
        back = pl.program_id(0) * together + k
        step = jnp.where(back < 2, back, 5 - back)
        place = lax.rem(where[1] + size - step, size)
        piece = made[k * share * slots : (k + 1) * share * slots]
        out_ref[pl.ds(place * share, share), 0] = piece.reshape(share, slots, columns).astype(
            out_ref.dtype
        )


def down_half(where, core, rows_in, weight, made, sources):
    rows, depth = rows_in.shape
    columns = weight.shape[2]
    slots = rows // sources
    tile = rows // 2
    in_specs = [
        pl.BlockSpec((tile, depth), lambda i, where: (i, 0)),
        pl.BlockSpec((None, depth, columns), lambda i, where: (0, 0, 0)),
    ]
    inputs = [rows_in, weight]
    aliases = {}
    if made is not None:
        in_specs.append(pl.BlockSpec(memory_space=pl.ANY))
        inputs.append(made)
        aliases = {3: 0}

    def half(i, where):
        return 0, where[0] + core - 2 * where[0] * core, 0, 0

    return pl.pallas_call(
        down_half_kernel,
        out_shape=jax.ShapeDtypeStruct((sources, 2, slots, columns), jnp.bfloat16),
        grid_spec=pltpu.PrefetchScalarGridSpec(
            num_scalar_prefetch=1,
            grid=(rows // tile,),
            in_specs=in_specs,
            out_specs=pl.BlockSpec((sources, 1, slots, columns), half),
        ),
        input_output_aliases=aliases,
        compiler_params=pltpu.CompilerParams(vmem_limit_bytes=VMEM),
        cost_estimate=cost(rows, depth, columns),
        name="down_half",
    )(where, *inputs)


def narrow_rows(where, rows_in, up, down):
    arrived = turned(their_half(where, rows_in, up), "role", 1)
    own, rounded = own_half(where, rows_in, up, arrived, 1)
    pieces = [turned(rounded, "tp", step) for step in (3, 1, 2)]
    for piece in pieces:
        own = own + piece.astype(jnp.float32)
    mine = jax.nn.silu(own).astype(jnp.bfloat16)
    return down_both(where, mine, turned(mine, "role", 1), down)


def wide_rows(where, rows_in, up, other_up, down, sources):
    size = lax.axis_size("tp")
    own, *pieces = wide_product(where, rows_in, up, other_up, size)
    for step in (3, 1, 2):
        own = own + turned(pieces[step - 1], "tp", step).astype(jnp.float32)
    mine = jax.nn.silu(own).astype(jnp.bfloat16)
    others = {step: turned(mine, "tp", step) for step in (3, 1, 2)}
    mine = jnp.concatenate([mine, others[1], others[3], others[2]], axis=0)
    theirs = turned(mine, "role", 1)
    made = down_half(where, 0, mine, down, None, sources)
    return down_half(where, 1, theirs, down, made, sources)


def shards(
    q_latent,
    key_value_cache,
    cache_lengths,
    hidden,
    expert_ids,
    route_logits,
    up_weight,
    down_weight,
):
    rows, width = hidden.shape
    owners = lax.axis_size("grp")
    experts = jnp.arange(EXPERTS, dtype=jnp.int32)
    where = jnp.stack([lax.axis_index("role"), lax.axis_index("tp")]).astype(jnp.int32)

    rank, first_out = first_selection(expert_ids, hidden)

    def exchanged(value):
        return lax.all_to_all(value, "grp", split_axis=0, concat_axis=0, tiled=True)

    def outgoing(first, count, source):
        slots = (first + jnp.arange(count, dtype=jnp.int32)).astype(jnp.float32)
        placed = rank[:, None, :] == slots[None, :, None]
        placed = placed.reshape(-1, rows).astype(jnp.bfloat16)
        made = jnp.dot(placed, source, preferred_element_type=jnp.float32).astype(jnp.bfloat16)
        return made.reshape(owners, count, source.shape[1])

    def weights(first, last):
        slots = jnp.arange(first, last, dtype=jnp.int32).astype(jnp.float32)
        taken = rank.T[:, :, None] == slots[None, None, :]
        return jnp.where(taken, weight_of[:, :, None], 0.0).reshape(rows, -1).astype(jnp.bfloat16)

    first_out, hidden = lax.optimization_barrier((first_out, hidden))
    first_in = exchanged(first_out)

    wide = jnp.concatenate([hidden, turned(hidden, "role", 1)], axis=1)
    passed_up = copied(up_weight[0])

    sigmoid_terms = jax.nn.sigmoid(route_logits)
    route_weights = 2.5 * sigmoid_terms / jnp.sum(sigmoid_terms, axis=-1, keepdims=True)
    named = expert_ids[:, None, :] == experts[None, :, None]
    weight_of = jnp.sum(jnp.where(named, route_weights[:, None, :], 0.0), axis=2)
    weights_of = [weights(0, FIRST), weights(FIRST, CAP)]

    half = (CAP - FIRST) // 2
    begin = FIRST + where[0] * half
    second_out, first_in, passed_up, *weights_of = lax.optimization_barrier(
        (outgoing(begin, half, wide), first_in, passed_up, *weights_of)
    )
    second_in = exchanged(second_out)
    other_up = turned(passed_up, "role", 1)
    first_out = narrow_rows(where, first_in.reshape(-1, width), up_weight[0], down_weight)
    second_in, first_out = lax.optimization_barrier((second_in, first_out))
    first_back = exchanged(first_out.reshape(owners, FIRST, width))
    second_out = wide_rows(where, second_in.reshape(-1, 2 * width), up_weight[0], other_up, down_weight, owners)
    second_out, first_back, q_latent = lax.optimization_barrier((second_out, first_back, q_latent))
    second_back = exchanged(second_out)

    packed = attention_part(q_latent, key_value_cache, cache_lengths)
    size = lax.axis_size("tp")
    heads = q_latent.shape[1] // size
    place = lax.axis_index("tp")
    pieces = [
        lax.dynamic_slice_in_dim(packed, (place + step) % size * heads, heads, 1)
        for step in range(size)
    ]
    pieces = [pieces[0]] + [turned(pieces[step], "tp", step) for step in (2, 1, 3)]
    attn_context = attention_join(pieces)
    first_back = first_back.reshape(-1, width)
    second_back = second_back.reshape(-1, width)
    result = combined(weights_of[0], first_back)
    result = result + jnp.dot(weights_of[1], second_back, preferred_element_type=jnp.float32)
    return (attn_context, result.astype(jnp.bfloat16))


def solution(mesh):
    return jax.shard_map(
        shards,
        mesh=mesh,
        in_specs=(
            P(("role", "grp"), None, None),
            P(("role", "grp"), "tp", None),
            P(("role", "grp")),
            P("grp", ("role", "tp")),
            P("grp", None),
            P("grp", None),
            P("grp", ("role", "tp"), None),
            P("grp", None, ("role", "tp")),
        ),
        out_specs=(P(("role", "grp"), "tp", None), P("grp", ("role", "tp"))),
        check_vma=False,
    )
```

```python
import functools

import jax
import jax.numpy as jnp
from jax import lax
from jax.experimental import pallas as pl
from jax.experimental.pallas import tpu as pltpu
from jax.sharding import PartitionSpec as P

KEY_VALUE_LATENT = 512
ROPE = 64
QK_NOPE = 128
EXPERTS = 64
CAP = 24
FIRST = 8
VMEM = 32 * 1024 * 1024
MOST = 60 * 1024 * 1024
LANES = 128

NEGATIVE = -1e30


def two_halves(value):
    high = value.astype(jnp.bfloat16)
    low = (value - high.astype(jnp.float32)).astype(jnp.bfloat16)
    return high, low


def attention_part(q_latent, key_value_cache, cache_lengths):
    score_scale = 1.0 / (QK_NOPE + ROPE) ** 0.5
    local_len = key_value_cache.shape[1]
    offset = lax.axis_index("tp") * local_len
    positions = offset + jnp.arange(local_len, dtype=jnp.int32)
    is_valid = positions[None, None, :] < cache_lengths[:, None, None]
    scores = (
        jnp.einsum("rhc,rlc->rhl", q_latent, key_value_cache, preferred_element_type=jnp.float32)
        * score_scale
    )
    scores = jnp.where(is_valid, scores, NEGATIVE)
    shift = jnp.max(scores, axis=-1).astype(jnp.bfloat16)
    exp_terms = jnp.where(
        is_valid, jnp.exp(scores - shift.astype(jnp.float32)[..., None]), 0.0
    )
    row_total = jnp.sum(exp_terms, axis=-1)
    context_total = jnp.einsum(
        "wzj,wjp->wzp",
        exp_terms.astype(jnp.bfloat16),
        key_value_cache[:, :, :KEY_VALUE_LATENT],
        preferred_element_type=jnp.float32,
    )
    total_high, total_low = two_halves(row_total)
    stats = jnp.stack([shift, total_high, total_low], axis=-1)
    stats = jnp.pad(stats, ((0, 0), (0, 0), (0, LANES - stats.shape[-1])))
    return jnp.concatenate([context_total.astype(jnp.bfloat16), stats], axis=-1)


def attention_join(pieces):
    mine = jnp.stack(pieces)
    context = mine[..., :KEY_VALUE_LATENT].astype(jnp.float32)
    stats = mine[..., KEY_VALUE_LATENT : KEY_VALUE_LATENT + 3].astype(jnp.float32)
    shift = stats[..., 0]
    total = stats[..., 1] + stats[..., 2]
    factor = jnp.exp(shift - jnp.max(shift, axis=0, keepdims=True))
    total_all = jnp.sum(total * factor, axis=0)
    context_all = jnp.sum(context * factor[..., None], axis=0)
    return (context_all / total_all[..., None]).astype(jnp.bfloat16)


def turned(value, axis, step):
    size = lax.axis_size(axis)
    return lax.ppermute(value, axis, [(k, (k + step) % size) for k in range(size)])


def cost(rows, depth, columns):
    return pl.CostEstimate(
        flops=2 * rows * depth * columns,
        bytes_accessed=2 * (rows * depth + depth * columns + rows * columns),
        transcendentals=0,
    )


def select_kernel(ids_ref, rows_ref, rank_ref, out_ref):
    top, rows = ids_ref.shape
    experts, slots, columns = out_ref.shape
    named = jnp.zeros((experts, rows), jnp.float32)
    numbers = lax.broadcasted_iota(jnp.int32, (experts, rows), 0)
    for k in range(top):
        named = jnp.where(ids_ref[k : k + 1, :] == numbers, 1.0, named)
    above = lax.broadcasted_iota(jnp.int32, (rows, rows), 0)
    right = lax.broadcasted_iota(jnp.int32, (rows, rows), 1)
    before = jnp.dot(
        named.astype(jnp.bfloat16),
        jnp.where(above < right, 1.0, 0.0).astype(jnp.bfloat16),
        preferred_element_type=jnp.float32,
    )
    rank = jnp.where(named > 0.5, before, -1.0)
    rank_ref[...] = rank
    slot = lax.broadcasted_iota(jnp.int32, (experts, slots, rows), 1).astype(jnp.float32)
    placed = jnp.where(rank[:, None, :] == slot, 1.0, 0.0).reshape(experts * slots, rows)
    made = jnp.dot(
        placed.astype(jnp.bfloat16), rows_ref[...], preferred_element_type=jnp.float32
    )
    out_ref[...] = made.reshape(experts, slots, columns).astype(out_ref.dtype)


def first_selection(ids, rows_in):
    rows, columns = rows_in.shape
    return pl.pallas_call(
        select_kernel,
        out_shape=[
            jax.ShapeDtypeStruct((EXPERTS, rows), jnp.float32),
            jax.ShapeDtypeStruct((EXPERTS, FIRST, columns), jnp.bfloat16),
        ],
        compiler_params=pltpu.CompilerParams(vmem_limit_bytes=MOST),
        cost_estimate=cost(EXPERTS * FIRST, rows, columns),
        name="first_selection",
    )(ids.T, rows_in)


def their_kernel(where, rows_ref, weight_ref, out_ref):
    out_ref[...] = jnp.dot(
        rows_ref[...], weight_ref[...], preferred_element_type=jnp.float32
    ).astype(out_ref.dtype)


def their_half(where, rows_in, weight):
    half, depth = rows_in.shape[0] // 2, rows_in.shape[1]
    columns = weight.shape[1]
    tile = min(256, half)
    steps = half // tile
    return pl.pallas_call(
        their_kernel,
        out_shape=jax.ShapeDtypeStruct((half, columns), jnp.bfloat16),
        grid_spec=pltpu.PrefetchScalarGridSpec(
            num_scalar_prefetch=1,
            grid=(steps,),
            in_specs=[
                pl.BlockSpec((tile, depth), lambda i, where: ((1 - where[0]) * steps + i, 0)),
                pl.BlockSpec((depth, columns), lambda i, where: (0, 0)),
            ],
            out_specs=pl.BlockSpec((tile, columns), lambda i, where: (i, 0)),
        ),
        compiler_params=pltpu.CompilerParams(vmem_limit_bytes=VMEM),
        cost_estimate=cost(half, depth, columns),
        name="their_half",
    )(where, rows_in, weight)


def own_kernel(where, rows_ref, weight_ref, arrived_ref, own_ref, *rest):
    piece_refs, total = rest[:-1], rest[-1]
    tile = rows_ref.shape[0]
    share = own_ref.shape[0]
    size = total.shape[0] // share
    step = pl.program_id(0)
    here = pl.ds(pl.multiple_of(step * tile, tile), tile)
    total[here, :] = jnp.dot(
        rows_ref[...], weight_ref[...], preferred_element_type=jnp.float32
    ) + arrived_ref[...].astype(jnp.float32)

    @pl.when(step == pl.num_programs(0) - 1)
    def _():
        if size == 1:
            own_ref[...] = total[...]
            piece_refs[0][...] = total[...].astype(jnp.bfloat16)
        else:
            for ahead in range(size):
                place = lax.rem(where[1] + ahead, size)
                piece = total[pl.ds(pl.multiple_of(place * share, share), share), :]
                if ahead == 0:
                    own_ref[...] = piece
                else:
                    piece_refs[ahead - 1][...] = piece.astype(jnp.bfloat16)


def own_half(where, rows_in, weight, arrived, size):
    half, depth = rows_in.shape[0] // 2, rows_in.shape[1]
    columns = weight.shape[1]
    tile = min(256, half)
    steps = half // tile
    share = half // size
    return pl.pallas_call(
        own_kernel,
        out_shape=[jax.ShapeDtypeStruct((share, columns), jnp.float32)]
        + [jax.ShapeDtypeStruct((share, columns), jnp.bfloat16)] * max(1, size - 1),
        grid_spec=pltpu.PrefetchScalarGridSpec(
            num_scalar_prefetch=1,
            grid=(steps,),
            in_specs=[
                pl.BlockSpec((tile, depth), lambda i, where: (where[0] * steps + i, 0)),
                pl.BlockSpec((depth, columns), lambda i, where: (0, 0)),
                pl.BlockSpec((tile, columns), lambda i, where: (i, 0)),
            ],
            out_specs=[pl.BlockSpec((share, columns), lambda i, where: (0, 0))]
            * max(2, size),
            scratch_shapes=[pltpu.VMEM((half, columns), jnp.float32)],
        ),
        compiler_params=pltpu.CompilerParams(vmem_limit_bytes=VMEM),
        cost_estimate=cost(half, depth, columns),
        name="own_half",
    )(where, rows_in, weight, arrived)


def combine_kernel(weights_ref, rows_ref, out_ref):
    out_ref[...] = jnp.dot(weights_ref[...], rows_ref[...], preferred_element_type=jnp.float32)


def combined(weights, rows_in):
    rows, depth = weights.shape
    columns = rows_in.shape[1]
    return pl.pallas_call(
        combine_kernel,
        out_shape=jax.ShapeDtypeStruct((rows, columns), jnp.float32),
        compiler_params=pltpu.CompilerParams(vmem_limit_bytes=MOST),
        cost_estimate=cost(rows, depth, columns),
        name="combined",
    )(weights, rows_in)


def copy_kernel(from_ref, to_ref):
    to_ref[...] = from_ref[...]


def copied(value):
    rows, columns = value.shape
    tile = 128
    return pl.pallas_call(
        copy_kernel,
        out_shape=jax.ShapeDtypeStruct(value.shape, value.dtype),
        grid=(rows // tile,),
        in_specs=[pl.BlockSpec((tile, columns), lambda i: (i, 0))],
        out_specs=pl.BlockSpec((tile, columns), lambda i: (i, 0)),
        compiler_params=pltpu.CompilerParams(vmem_limit_bytes=VMEM),
        cost_estimate=pl.CostEstimate(
            flops=0, bytes_accessed=4 * rows * columns, transcendentals=0
        ),
        name="copied",
    )(value)


def down_kernel(where, mine_ref, theirs_ref, weight_ref, out_ref):
    @pl.when(pl.program_id(0) == 0)
    def _():
        out_ref[...] = jnp.dot(
            mine_ref[...], weight_ref[...], preferred_element_type=jnp.float32
        ).astype(out_ref.dtype)

    @pl.when(pl.program_id(0) == 1)
    def _():
        out_ref[...] = jnp.dot(
            theirs_ref[...], weight_ref[...], preferred_element_type=jnp.float32
        ).astype(out_ref.dtype)


def down_both(where, mine, theirs, weight):
    half, depth = mine.shape
    columns = weight.shape[2]
    return pl.pallas_call(
        down_kernel,
        out_shape=jax.ShapeDtypeStruct((2 * half, columns), jnp.bfloat16),
        grid_spec=pltpu.PrefetchScalarGridSpec(
            num_scalar_prefetch=1,
            grid=(2,),
            in_specs=[
                pl.BlockSpec((half, depth), lambda h, where: (0, 0)),
                pl.BlockSpec((half, depth), lambda h, where: (0, 0)),
                pl.BlockSpec((None, depth, columns), lambda h, where: (0, 0, 0)),
            ],
            out_specs=pl.BlockSpec(
                (half, columns), lambda h, where: (where[0] + h - 2 * where[0] * h, 0)
            ),
        ),
        compiler_params=pltpu.CompilerParams(vmem_limit_bytes=VMEM),
        cost_estimate=cost(2 * half, depth, columns),
        name="down_both",
    )(where, mine, theirs, weight)


def wide_kernel(where, rows_ref, weight_ref, other_ref, *out_refs):
    depth = weight_ref.shape[0]
    share = out_refs[0].shape[0]
    size = len(out_refs)
    for ahead, out_ref in enumerate(out_refs):
        place = lax.rem(where[1] + ahead, size)
        rows = rows_ref[pl.ds(pl.multiple_of(place * share, share), share), :]
        made = jnp.dot(
            rows[:, :depth], weight_ref[...], preferred_element_type=jnp.float32
        ) + jnp.dot(rows[:, depth:], other_ref[...], preferred_element_type=jnp.float32)
        out_ref[...] = made.astype(out_ref.dtype)


def wide_product(where, rows_in, weight, other, size):
    rows, width = rows_in.shape
    depth, columns = weight.shape
    share = rows // size
    return pl.pallas_call(
        wide_kernel,
        out_shape=[jax.ShapeDtypeStruct((share, columns), jnp.float32)]
        + [jax.ShapeDtypeStruct((share, columns), jnp.bfloat16)] * (size - 1),
        grid_spec=pltpu.PrefetchScalarGridSpec(
            num_scalar_prefetch=1,
            grid=(1,),
            in_specs=[
                pl.BlockSpec((rows, width), lambda i, where: (0, 0)),
                pl.BlockSpec((depth, columns), lambda i, where: (0, 0)),
                pl.BlockSpec((depth, columns), lambda i, where: (0, 0)),
            ],
            out_specs=[pl.BlockSpec((share, columns), lambda i, where: (0, 0))] * size,
        ),
        compiler_params=pltpu.CompilerParams(vmem_limit_bytes=VMEM),
        cost_estimate=cost(rows, width, columns),
        name="wide_product",
    )(where, rows_in, weight, other)


def down_half_kernel(where, rows_ref, weight_ref, *rest):
    out_ref = rest[-1]
    sources, _, slots, columns = out_ref.shape
    size = 4
    share = sources // size
    together = rows_ref.shape[0] // (share * slots)
    made = jnp.dot(rows_ref[...], weight_ref[...], preferred_element_type=jnp.float32)
    for k in range(together):
        back = pl.program_id(0) * together + k
        step = jnp.where(back < 2, back, 5 - back)
        place = lax.rem(where[1] + size - step, size)
        piece = made[k * share * slots : (k + 1) * share * slots]
        out_ref[pl.ds(place * share, share), 0] = piece.reshape(share, slots, columns).astype(
            out_ref.dtype
        )


def down_half(where, core, rows_in, weight, made, sources):
    rows, depth = rows_in.shape
    columns = weight.shape[2]
    slots = rows // sources
    tile = rows // 2
    in_specs = [
        pl.BlockSpec((tile, depth), lambda i, where: (i, 0)),
        pl.BlockSpec((None, depth, columns), lambda i, where: (0, 0, 0)),
    ]
    inputs = [rows_in, weight]
    aliases = {}
    if made is not None:
        in_specs.append(pl.BlockSpec(memory_space=pl.ANY))
        inputs.append(made)
        aliases = {3: 0}

    def half(i, where):
        return 0, where[0] + core - 2 * where[0] * core, 0, 0

    return pl.pallas_call(
        down_half_kernel,
        out_shape=jax.ShapeDtypeStruct((sources, 2, slots, columns), jnp.bfloat16),
        grid_spec=pltpu.PrefetchScalarGridSpec(
            num_scalar_prefetch=1,
            grid=(rows // tile,),
            in_specs=in_specs,
            out_specs=pl.BlockSpec((sources, 1, slots, columns), half),
        ),
        input_output_aliases=aliases,
        compiler_params=pltpu.CompilerParams(vmem_limit_bytes=VMEM),
        cost_estimate=cost(rows, depth, columns),
        name="down_half",
    )(where, *inputs)


def narrow_rows(where, rows_in, up, down):
    arrived = turned(their_half(where, rows_in, up), "role", 1)
    own, rounded = own_half(where, rows_in, up, arrived, 1)
    pieces = [turned(rounded, "tp", step) for step in (3, 1, 2)]
    for piece in pieces:
        own = own + piece.astype(jnp.float32)
    mine = jax.nn.silu(own).astype(jnp.bfloat16)
    return down_both(where, mine, turned(mine, "role", 1), down)


def wide_rows(where, rows_in, up, other_up, down, sources):
    size = lax.axis_size("tp")
    own, *pieces = wide_product(where, rows_in, up, other_up, size)
    for step in (2, 1, 3):
        own = own + turned(pieces[step - 1], "tp", step).astype(jnp.float32)
    mine = jax.nn.silu(own).astype(jnp.bfloat16)
    others = {step: turned(mine, "tp", step) for step in (3, 1, 2)}
    mine = jnp.concatenate([mine, others[1], others[3], others[2]], axis=0)
    theirs = turned(mine, "role", 1)
    made = down_half(where, 0, mine, down, None, sources)
    return down_half(where, 1, theirs, down, made, sources)


def shards(
    q_latent,
    key_value_cache,
    cache_lengths,
    hidden,
    expert_ids,
    route_logits,
    up_weight,
    down_weight,
):
    rows, width = hidden.shape
    owners = lax.axis_size("grp")
    experts = jnp.arange(EXPERTS, dtype=jnp.int32)
    where = jnp.stack([lax.axis_index("role"), lax.axis_index("tp")]).astype(jnp.int32)

    rank, first_out = first_selection(expert_ids, hidden)

    def exchanged(value):
        return lax.all_to_all(value, "grp", split_axis=0, concat_axis=0, tiled=True)

    def outgoing(first, count, source):
        slots = (first + jnp.arange(count, dtype=jnp.int32)).astype(jnp.float32)
        placed = rank[:, None, :] == slots[None, :, None]
        placed = placed.reshape(-1, rows).astype(jnp.bfloat16)
        made = jnp.dot(placed, source, preferred_element_type=jnp.float32).astype(jnp.bfloat16)
        return made.reshape(owners, count, source.shape[1])

    def weights(first, last):
        slots = jnp.arange(first, last, dtype=jnp.int32).astype(jnp.float32)
        taken = rank.T[:, :, None] == slots[None, None, :]
        return jnp.where(taken, weight_of[:, :, None], 0.0).reshape(rows, -1).astype(jnp.bfloat16)

    first_out, hidden = lax.optimization_barrier((first_out, hidden))
    first_in = exchanged(first_out)

    wide = jnp.concatenate([hidden, turned(hidden, "role", 1)], axis=1)
    passed_up = copied(up_weight[0])

    sigmoid_terms = jax.nn.sigmoid(route_logits)
    route_weights = 2.5 * sigmoid_terms / jnp.sum(sigmoid_terms, axis=-1, keepdims=True)
    named = expert_ids[:, None, :] == experts[None, :, None]
    weight_of = jnp.sum(jnp.where(named, route_weights[:, None, :], 0.0), axis=2)
    weights_of = [weights(0, FIRST), weights(FIRST, CAP)]

    half = (CAP - FIRST) // 2
    begin = FIRST + where[0] * half
    second_out, first_in, passed_up, *weights_of = lax.optimization_barrier(
        (outgoing(begin, half, wide), first_in, passed_up, *weights_of)
    )
    second_in = exchanged(second_out)
    other_up = turned(passed_up, "role", 1)
    first_out = narrow_rows(where, first_in.reshape(-1, width), up_weight[0], down_weight)
    second_in, first_out = lax.optimization_barrier((second_in, first_out))
    first_back = exchanged(first_out.reshape(owners, FIRST, width))
    second_out = wide_rows(where, second_in.reshape(-1, 2 * width), up_weight[0], other_up, down_weight, owners)
    second_out, first_back, q_latent = lax.optimization_barrier((second_out, first_back, q_latent))
    second_back = exchanged(second_out)

    packed = attention_part(q_latent, key_value_cache, cache_lengths)
    size = lax.axis_size("tp")
    heads = q_latent.shape[1] // size
    place = lax.axis_index("tp")
    pieces = [
        lax.dynamic_slice_in_dim(packed, (place + step) % size * heads, heads, 1)
        for step in range(size)
    ]
    pieces = [pieces[0]] + [turned(pieces[step], "tp", step) for step in (2, 1, 3)]
    attn_context = attention_join(pieces)
    first_back = first_back.reshape(-1, width)
    second_back = second_back.reshape(-1, width)
    result = combined(weights_of[0], first_back)
    result = result + jnp.dot(weights_of[1], second_back, preferred_element_type=jnp.float32)
    return (attn_context, result.astype(jnp.bfloat16))


def solution(mesh):
    return jax.shard_map(
        shards,
        mesh=mesh,
        in_specs=(
            P(("role", "grp"), None, None),
            P(("role", "grp"), "tp", None),
            P(("role", "grp")),
            P("grp", ("role", "tp")),
            P("grp", None),
            P("grp", None),
            P("grp", ("role", "tp"), None),
            P("grp", None, ("role", "tp")),
        ),
        out_specs=(P(("role", "grp"), "tp", None), P("grp", ("role", "tp"))),
        check_vma=False,
    )
```

```python
import functools

import jax
import jax.numpy as jnp
from jax import lax
from jax.experimental import pallas as pl
from jax.experimental.pallas import tpu as pltpu
from jax.sharding import PartitionSpec as P

KEY_VALUE_LATENT = 512
ROPE = 64
QK_NOPE = 128
EXPERTS = 64
CAP = 24
FIRST = 8
VMEM = 32 * 1024 * 1024
MOST = 60 * 1024 * 1024
LANES = 128

NEGATIVE = -1e30


def two_halves(value):
    high = value.astype(jnp.bfloat16)
    low = (value - high.astype(jnp.float32)).astype(jnp.bfloat16)
    return high, low


def attention_part(q_latent, key_value_cache, cache_lengths):
    score_scale = 1.0 / (QK_NOPE + ROPE) ** 0.5
    local_len = key_value_cache.shape[1]
    offset = lax.axis_index("tp") * local_len
    positions = offset + jnp.arange(local_len, dtype=jnp.int32)
    is_valid = positions[None, None, :] < cache_lengths[:, None, None]
    scores = (
        jnp.einsum("rhc,rlc->rhl", q_latent, key_value_cache, preferred_element_type=jnp.float32)
        * score_scale
    )
    scores = jnp.where(is_valid, scores, NEGATIVE)
    shift = jnp.max(scores, axis=-1).astype(jnp.bfloat16)
    exp_terms = jnp.where(
        is_valid, jnp.exp(scores - shift.astype(jnp.float32)[..., None]), 0.0
    )
    row_total = jnp.sum(exp_terms, axis=-1)
    context_total = jnp.einsum(
        "wzj,wjp->wzp",
        exp_terms.astype(jnp.bfloat16),
        key_value_cache[:, :, :KEY_VALUE_LATENT],
        preferred_element_type=jnp.float32,
    )
    total_high, total_low = two_halves(row_total)
    stats = jnp.stack([shift, total_high, total_low], axis=-1)
    stats = jnp.pad(stats, ((0, 0), (0, 0), (0, LANES - stats.shape[-1])))
    return jnp.concatenate([context_total.astype(jnp.bfloat16), stats], axis=-1)


def attention_join(pieces):
    mine = jnp.stack(pieces)
    context = mine[..., :KEY_VALUE_LATENT].astype(jnp.float32)
    stats = mine[..., KEY_VALUE_LATENT : KEY_VALUE_LATENT + 3].astype(jnp.float32)
    shift = stats[..., 0]
    total = stats[..., 1] + stats[..., 2]
    factor = jnp.exp(shift - jnp.max(shift, axis=0, keepdims=True))
    total_all = jnp.sum(total * factor, axis=0)
    context_all = jnp.sum(context * factor[..., None], axis=0)
    return (context_all / total_all[..., None]).astype(jnp.bfloat16)


def turned(value, axis, step):
    size = lax.axis_size(axis)
    return lax.ppermute(value, axis, [(k, (k + step) % size) for k in range(size)])


def cost(rows, depth, columns):
    return pl.CostEstimate(
        flops=2 * rows * depth * columns,
        bytes_accessed=2 * (rows * depth + depth * columns + rows * columns),
        transcendentals=0,
    )


def select_kernel(ids_ref, rows_ref, rank_ref, out_ref):
    top, rows = ids_ref.shape
    experts, slots, columns = out_ref.shape
    named = jnp.zeros((experts, rows), jnp.float32)
    numbers = lax.broadcasted_iota(jnp.int32, (experts, rows), 0) + pl.program_id(0) * experts
    for k in range(top):
        named = jnp.where(ids_ref[k : k + 1, :] == numbers, 1.0, named)
    above = lax.broadcasted_iota(jnp.int32, (rows, rows), 0)
    right = lax.broadcasted_iota(jnp.int32, (rows, rows), 1)
    before = jnp.dot(
        named.astype(jnp.bfloat16),
        jnp.where(above < right, 1.0, 0.0).astype(jnp.bfloat16),
        preferred_element_type=jnp.float32,
    )
    rank = jnp.where(named > 0.5, before, -1.0)
    rank_ref[...] = rank
    slot = lax.broadcasted_iota(jnp.int32, (experts, slots, rows), 1).astype(jnp.float32)
    placed = jnp.where(rank[:, None, :] == slot, 1.0, 0.0).reshape(experts * slots, rows)
    made = jnp.dot(
        placed.astype(jnp.bfloat16), rows_ref[...], preferred_element_type=jnp.float32
    )
    out_ref[...] = made.reshape(experts, slots, columns).astype(out_ref.dtype)


def first_selection(ids, rows_in):
    rows, columns = rows_in.shape
    top = ids.shape[1]
    together = EXPERTS // 4
    return pl.pallas_call(
        select_kernel,
        out_shape=[
            jax.ShapeDtypeStruct((EXPERTS, rows), jnp.float32),
            jax.ShapeDtypeStruct((EXPERTS, FIRST, columns), jnp.bfloat16),
        ],
        grid=(EXPERTS // together,),
        in_specs=[
            pl.BlockSpec((top, rows), lambda i: (0, 0)),
            pl.BlockSpec((rows, columns), lambda i: (0, 0)),
        ],
        out_specs=[
            pl.BlockSpec((together, rows), lambda i: (i, 0)),
            pl.BlockSpec((together, FIRST, columns), lambda i: (i, 0, 0)),
        ],
        compiler_params=pltpu.CompilerParams(vmem_limit_bytes=MOST),
        cost_estimate=cost(EXPERTS * FIRST, rows, columns),
        name="first_selection",
    )(ids.T, rows_in)


def their_kernel(where, rows_ref, weight_ref, out_ref):
    out_ref[...] = jnp.dot(
        rows_ref[...], weight_ref[...], preferred_element_type=jnp.float32
    ).astype(out_ref.dtype)


def their_half(where, rows_in, weight):
    half, depth = rows_in.shape[0] // 2, rows_in.shape[1]
    columns = weight.shape[1]
    tile = min(256, half)
    steps = half // tile
    return pl.pallas_call(
        their_kernel,
        out_shape=jax.ShapeDtypeStruct((half, columns), jnp.bfloat16),
        grid_spec=pltpu.PrefetchScalarGridSpec(
            num_scalar_prefetch=1,
            grid=(steps,),
            in_specs=[
                pl.BlockSpec((tile, depth), lambda i, where: ((1 - where[0]) * steps + i, 0)),
                pl.BlockSpec((depth, columns), lambda i, where: (0, 0)),
            ],
            out_specs=pl.BlockSpec((tile, columns), lambda i, where: (i, 0)),
        ),
        compiler_params=pltpu.CompilerParams(vmem_limit_bytes=VMEM),
        cost_estimate=cost(half, depth, columns),
        name="their_half",
    )(where, rows_in, weight)


def own_kernel(where, rows_ref, weight_ref, arrived_ref, own_ref, *rest):
    piece_refs, total = rest[:-1], rest[-1]
    tile = rows_ref.shape[0]
    share = own_ref.shape[0]
    size = total.shape[0] // share
    step = pl.program_id(0)
    here = pl.ds(pl.multiple_of(step * tile, tile), tile)
    total[here, :] = jnp.dot(
        rows_ref[...], weight_ref[...], preferred_element_type=jnp.float32
    ) + arrived_ref[...].astype(jnp.float32)

    @pl.when(step == pl.num_programs(0) - 1)
    def _():
        if size == 1:
            own_ref[...] = total[...]
            piece_refs[0][...] = total[...].astype(jnp.bfloat16)
        else:
            for ahead in range(size):
                place = lax.rem(where[1] + ahead, size)
                piece = total[pl.ds(pl.multiple_of(place * share, share), share), :]
                if ahead == 0:
                    own_ref[...] = piece
                else:
                    piece_refs[ahead - 1][...] = piece.astype(jnp.bfloat16)


def own_half(where, rows_in, weight, arrived, size):
    half, depth = rows_in.shape[0] // 2, rows_in.shape[1]
    columns = weight.shape[1]
    tile = min(256, half)
    steps = half // tile
    share = half // size
    return pl.pallas_call(
        own_kernel,
        out_shape=[jax.ShapeDtypeStruct((share, columns), jnp.float32)]
        + [jax.ShapeDtypeStruct((share, columns), jnp.bfloat16)] * max(1, size - 1),
        grid_spec=pltpu.PrefetchScalarGridSpec(
            num_scalar_prefetch=1,
            grid=(steps,),
            in_specs=[
                pl.BlockSpec((tile, depth), lambda i, where: (where[0] * steps + i, 0)),
                pl.BlockSpec((depth, columns), lambda i, where: (0, 0)),
                pl.BlockSpec((tile, columns), lambda i, where: (i, 0)),
            ],
            out_specs=[pl.BlockSpec((share, columns), lambda i, where: (0, 0))]
            * max(2, size),
            scratch_shapes=[pltpu.VMEM((half, columns), jnp.float32)],
        ),
        compiler_params=pltpu.CompilerParams(vmem_limit_bytes=VMEM),
        cost_estimate=cost(half, depth, columns),
        name="own_half",
    )(where, rows_in, weight, arrived)


def combine_kernel(weights_ref, rows_ref, out_ref):
    out_ref[...] = jnp.dot(weights_ref[...], rows_ref[...], preferred_element_type=jnp.float32)


def combined(weights, rows_in):
    rows, depth = weights.shape
    columns = rows_in.shape[1]
    return pl.pallas_call(
        combine_kernel,
        out_shape=jax.ShapeDtypeStruct((rows, columns), jnp.float32),
        compiler_params=pltpu.CompilerParams(vmem_limit_bytes=MOST),
        cost_estimate=cost(rows, depth, columns),
        name="combined",
    )(weights, rows_in)


def copy_kernel(from_ref, to_ref):
    to_ref[...] = from_ref[...]


def copied(value):
    rows, columns = value.shape
    tile = 128
    return pl.pallas_call(
        copy_kernel,
        out_shape=jax.ShapeDtypeStruct(value.shape, value.dtype),
        grid=(rows // tile,),
        in_specs=[pl.BlockSpec((tile, columns), lambda i: (i, 0))],
        out_specs=pl.BlockSpec((tile, columns), lambda i: (i, 0)),
        compiler_params=pltpu.CompilerParams(vmem_limit_bytes=VMEM),
        cost_estimate=pl.CostEstimate(
            flops=0, bytes_accessed=4 * rows * columns, transcendentals=0
        ),
        name="copied",
    )(value)


def down_kernel(where, mine_ref, theirs_ref, weight_ref, out_ref):
    @pl.when(pl.program_id(0) == 0)
    def _():
        out_ref[...] = jnp.dot(
            mine_ref[...], weight_ref[...], preferred_element_type=jnp.float32
        ).astype(out_ref.dtype)

    @pl.when(pl.program_id(0) == 1)
    def _():
        out_ref[...] = jnp.dot(
            theirs_ref[...], weight_ref[...], preferred_element_type=jnp.float32
        ).astype(out_ref.dtype)


def down_both(where, mine, theirs, weight):
    half, depth = mine.shape
    columns = weight.shape[2]
    return pl.pallas_call(
        down_kernel,
        out_shape=jax.ShapeDtypeStruct((2 * half, columns), jnp.bfloat16),
        grid_spec=pltpu.PrefetchScalarGridSpec(
            num_scalar_prefetch=1,
            grid=(2,),
            in_specs=[
                pl.BlockSpec((half, depth), lambda h, where: (0, 0)),
                pl.BlockSpec((half, depth), lambda h, where: (0, 0)),
                pl.BlockSpec((None, depth, columns), lambda h, where: (0, 0, 0)),
            ],
            out_specs=pl.BlockSpec(
                (half, columns), lambda h, where: (where[0] + h - 2 * where[0] * h, 0)
            ),
        ),
        compiler_params=pltpu.CompilerParams(vmem_limit_bytes=VMEM),
        cost_estimate=cost(2 * half, depth, columns),
        name="down_both",
    )(where, mine, theirs, weight)


def wide_kernel(where, rows_ref, weight_ref, other_ref, *out_refs):
    depth = weight_ref.shape[0]
    share = out_refs[0].shape[0]
    size = len(out_refs)
    for ahead, out_ref in enumerate(out_refs):
        place = lax.rem(where[1] + ahead, size)
        rows = rows_ref[pl.ds(pl.multiple_of(place * share, share), share), :]
        made = jnp.dot(
            rows[:, :depth], weight_ref[...], preferred_element_type=jnp.float32
        ) + jnp.dot(rows[:, depth:], other_ref[...], preferred_element_type=jnp.float32)
        out_ref[...] = made.astype(out_ref.dtype)


def wide_product(where, rows_in, weight, other, size):
    rows, width = rows_in.shape
    depth, columns = weight.shape
    share = rows // size
    return pl.pallas_call(
        wide_kernel,
        out_shape=[jax.ShapeDtypeStruct((share, columns), jnp.float32)]
        + [jax.ShapeDtypeStruct((share, columns), jnp.bfloat16)] * (size - 1),
        grid_spec=pltpu.PrefetchScalarGridSpec(
            num_scalar_prefetch=1,
            grid=(1,),
            in_specs=[
                pl.BlockSpec((rows, width), lambda i, where: (0, 0)),
                pl.BlockSpec((depth, columns), lambda i, where: (0, 0)),
                pl.BlockSpec((depth, columns), lambda i, where: (0, 0)),
            ],
            out_specs=[pl.BlockSpec((share, columns), lambda i, where: (0, 0))] * size,
        ),
        compiler_params=pltpu.CompilerParams(vmem_limit_bytes=VMEM),
        cost_estimate=cost(rows, width, columns),
        name="wide_product",
    )(where, rows_in, weight, other)


def down_half_kernel(where, rows_ref, weight_ref, *rest):
    out_ref = rest[-1]
    sources, _, slots, columns = out_ref.shape
    size = 4
    share = sources // size
    together = rows_ref.shape[0] // (share * slots)
    made = jnp.dot(rows_ref[...], weight_ref[...], preferred_element_type=jnp.float32)
    for k in range(together):
        back = pl.program_id(0) * together + k
        step = jnp.where(back < 2, back, 5 - back)
        place = lax.rem(where[1] + size - step, size)
        piece = made[k * share * slots : (k + 1) * share * slots]
        out_ref[pl.ds(place * share, share), 0] = piece.reshape(share, slots, columns).astype(
            out_ref.dtype
        )


def down_half(where, core, rows_in, weight, made, sources):
    rows, depth = rows_in.shape
    columns = weight.shape[2]
    slots = rows // sources
    tile = rows // 2
    in_specs = [
        pl.BlockSpec((tile, depth), lambda i, where: (i, 0)),
        pl.BlockSpec((None, depth, columns), lambda i, where: (0, 0, 0)),
    ]
    inputs = [rows_in, weight]
    aliases = {}
    if made is not None:
        in_specs.append(pl.BlockSpec(memory_space=pl.ANY))
        inputs.append(made)
        aliases = {3: 0}

    def half(i, where):
        return 0, where[0] + core - 2 * where[0] * core, 0, 0

    return pl.pallas_call(
        down_half_kernel,
        out_shape=jax.ShapeDtypeStruct((sources, 2, slots, columns), jnp.bfloat16),
        grid_spec=pltpu.PrefetchScalarGridSpec(
            num_scalar_prefetch=1,
            grid=(rows // tile,),
            in_specs=in_specs,
            out_specs=pl.BlockSpec((sources, 1, slots, columns), half),
        ),
        input_output_aliases=aliases,
        compiler_params=pltpu.CompilerParams(vmem_limit_bytes=VMEM),
        cost_estimate=cost(rows, depth, columns),
        name="down_half",
    )(where, *inputs)


def narrow_rows(where, rows_in, up, down):
    arrived = turned(their_half(where, rows_in, up), "role", 1)
    own, rounded = own_half(where, rows_in, up, arrived, 1)
    pieces = [turned(rounded, "tp", step) for step in (3, 1, 2)]
    for piece in pieces:
        own = own + piece.astype(jnp.float32)
    mine = jax.nn.silu(own).astype(jnp.bfloat16)
    return down_both(where, mine, turned(mine, "role", 1), down)


def wide_rows(where, rows_in, up, other_up, down, sources):
    size = lax.axis_size("tp")
    own, *pieces = wide_product(where, rows_in, up, other_up, size)
    for step in (3, 1, 2):
        own = own + turned(pieces[step - 1], "tp", step).astype(jnp.float32)
    mine = jax.nn.silu(own).astype(jnp.bfloat16)
    others = {step: turned(mine, "tp", step) for step in (3, 1, 2)}
    mine = jnp.concatenate([mine, others[1], others[3], others[2]], axis=0)
    theirs = turned(mine, "role", 1)
    made = down_half(where, 0, mine, down, None, sources)
    return down_half(where, 1, theirs, down, made, sources)


def shards(
    q_latent,
    key_value_cache,
    cache_lengths,
    hidden,
    expert_ids,
    route_logits,
    up_weight,
    down_weight,
):
    rows, width = hidden.shape
    owners = lax.axis_size("grp")
    experts = jnp.arange(EXPERTS, dtype=jnp.int32)
    where = jnp.stack([lax.axis_index("role"), lax.axis_index("tp")]).astype(jnp.int32)

    rank, first_out = first_selection(expert_ids, hidden)

    def exchanged(value):
        return lax.all_to_all(value, "grp", split_axis=0, concat_axis=0, tiled=True)

    def outgoing(first, count, source):
        slots = (first + jnp.arange(count, dtype=jnp.int32)).astype(jnp.float32)
        placed = rank[:, None, :] == slots[None, :, None]
        placed = placed.reshape(-1, rows).astype(jnp.bfloat16)
        made = jnp.dot(placed, source, preferred_element_type=jnp.float32).astype(jnp.bfloat16)
        return made.reshape(owners, count, source.shape[1])

    def weights(first, last):
        slots = jnp.arange(first, last, dtype=jnp.int32).astype(jnp.float32)
        taken = rank.T[:, :, None] == slots[None, None, :]
        return jnp.where(taken, weight_of[:, :, None], 0.0).reshape(rows, -1).astype(jnp.bfloat16)

    first_out, hidden = lax.optimization_barrier((first_out, hidden))
    first_in = exchanged(first_out)

    wide = jnp.concatenate([hidden, turned(hidden, "role", 1)], axis=1)
    passed_up = copied(up_weight[0])

    sigmoid_terms = jax.nn.sigmoid(route_logits)
    route_weights = 2.5 * sigmoid_terms / jnp.sum(sigmoid_terms, axis=-1, keepdims=True)
    named = expert_ids[:, None, :] == experts[None, :, None]
    weight_of = jnp.sum(jnp.where(named, route_weights[:, None, :], 0.0), axis=2)
    weights_of = [weights(0, FIRST), weights(FIRST, CAP)]

    half = (CAP - FIRST) // 2
    begin = FIRST + where[0] * half
    second_out, first_in, passed_up, *weights_of = lax.optimization_barrier(
        (outgoing(begin, half, wide), first_in, passed_up, *weights_of)
    )
    second_in = exchanged(second_out)
    other_up = turned(passed_up, "role", 1)
    first_out = narrow_rows(where, first_in.reshape(-1, width), up_weight[0], down_weight)
    second_in, first_out = lax.optimization_barrier((second_in, first_out))
    first_back = exchanged(first_out.reshape(owners, FIRST, width))
    second_out = wide_rows(where, second_in.reshape(-1, 2 * width), up_weight[0], other_up, down_weight, owners)
    second_out, first_back, q_latent = lax.optimization_barrier((second_out, first_back, q_latent))
    second_back = exchanged(second_out)

    packed = attention_part(q_latent, key_value_cache, cache_lengths)
    size = lax.axis_size("tp")
    heads = q_latent.shape[1] // size
    place = lax.axis_index("tp")
    pieces = [
        lax.dynamic_slice_in_dim(packed, (place + step) % size * heads, heads, 1)
        for step in range(size)
    ]
    pieces = [pieces[0]] + [turned(pieces[step], "tp", step) for step in (2, 1, 3)]
    attn_context = attention_join(pieces)
    first_back = first_back.reshape(-1, width)
    second_back = second_back.reshape(-1, width)
    result = combined(weights_of[0], first_back)
    result = result + jnp.dot(weights_of[1], second_back, preferred_element_type=jnp.float32)
    return (attn_context, result.astype(jnp.bfloat16))


def solution(mesh):
    return jax.shard_map(
        shards,
        mesh=mesh,
        in_specs=(
            P(("role", "grp"), None, None),
            P(("role", "grp"), "tp", None),
            P(("role", "grp")),
            P("grp", ("role", "tp")),
            P("grp", None),
            P("grp", None),
            P("grp", ("role", "tp"), None),
            P("grp", None, ("role", "tp")),
        ),
        out_specs=(P(("role", "grp"), "tp", None), P("grp", ("role", "tp"))),
        check_vma=False,
    )
```

```python
import functools

import jax
import jax.numpy as jnp
from jax import lax
from jax.experimental import pallas as pl
from jax.experimental.pallas import tpu as pltpu
from jax.sharding import PartitionSpec as P

KEY_VALUE_LATENT = 512
ROPE = 64
QK_NOPE = 128
EXPERTS = 64
CAP = 24
FIRST = 8
VMEM = 32 * 1024 * 1024
MOST = 60 * 1024 * 1024
LANES = 128

NEGATIVE = -1e30


def two_halves(value):
    high = value.astype(jnp.bfloat16)
    low = (value - high.astype(jnp.float32)).astype(jnp.bfloat16)
    return high, low


def attention_part(q_latent, key_value_cache, cache_lengths):
    score_scale = 1.0 / (QK_NOPE + ROPE) ** 0.5
    local_len = key_value_cache.shape[1]
    offset = lax.axis_index("tp") * local_len
    positions = offset + jnp.arange(local_len, dtype=jnp.int32)
    is_valid = positions[None, None, :] < cache_lengths[:, None, None]
    scores = (
        jnp.einsum("rhc,rlc->rhl", q_latent, key_value_cache, preferred_element_type=jnp.float32)
        * score_scale
    )
    scores = jnp.where(is_valid, scores, NEGATIVE)
    shift = jnp.max(scores, axis=-1).astype(jnp.bfloat16)
    exp_terms = jnp.where(
        is_valid, jnp.exp(scores - shift.astype(jnp.float32)[..., None]), 0.0
    )
    row_total = jnp.sum(exp_terms, axis=-1)
    context_total = jnp.einsum(
        "wzj,wjp->wzp",
        exp_terms.astype(jnp.bfloat16),
        key_value_cache[:, :, :KEY_VALUE_LATENT],
        preferred_element_type=jnp.float32,
    )
    total_high, total_low = two_halves(row_total)
    stats = jnp.stack([shift, total_high, total_low], axis=-1)
    stats = jnp.pad(stats, ((0, 0), (0, 0), (0, LANES - stats.shape[-1])))
    return jnp.concatenate([context_total.astype(jnp.bfloat16), stats], axis=-1)


def attention_join(pieces):
    mine = jnp.stack(pieces)
    context = mine[..., :KEY_VALUE_LATENT].astype(jnp.float32)
    stats = mine[..., KEY_VALUE_LATENT : KEY_VALUE_LATENT + 3].astype(jnp.float32)
    shift = stats[..., 0]
    total = stats[..., 1] + stats[..., 2]
    factor = jnp.exp(shift - jnp.max(shift, axis=0, keepdims=True))
    total_all = jnp.sum(total * factor, axis=0)
    context_all = jnp.sum(context * factor[..., None], axis=0)
    return (context_all / total_all[..., None]).astype(jnp.bfloat16)


def turned(value, axis, step):
    size = lax.axis_size(axis)
    return lax.ppermute(value, axis, [(k, (k + step) % size) for k in range(size)])


def cost(rows, depth, columns):
    return pl.CostEstimate(
        flops=2 * rows * depth * columns,
        bytes_accessed=2 * (rows * depth + depth * columns + rows * columns),
        transcendentals=0,
    )


def select_kernel(ids_ref, rows_ref, rank_ref, out_ref):
    top, rows = ids_ref.shape
    experts, slots, columns = out_ref.shape
    named = jnp.zeros((experts, rows), jnp.float32)
    numbers = lax.broadcasted_iota(jnp.int32, (experts, rows), 0)
    for k in range(top):
        named = jnp.where(ids_ref[k : k + 1, :] == numbers, 1.0, named)
    above = lax.broadcasted_iota(jnp.int32, (rows, rows), 0)
    right = lax.broadcasted_iota(jnp.int32, (rows, rows), 1)
    before = jnp.dot(
        named.astype(jnp.bfloat16),
        jnp.where(above < right, 1.0, 0.0).astype(jnp.bfloat16),
        preferred_element_type=jnp.float32,
    )
    rank = jnp.where(named > 0.5, before, -1.0)
    rank_ref[...] = rank
    slot = lax.broadcasted_iota(jnp.int32, (experts, slots, rows), 1).astype(jnp.float32)
    placed = jnp.where(rank[:, None, :] == slot, 1.0, 0.0).reshape(experts * slots, rows)
    made = jnp.dot(
        placed.astype(jnp.bfloat16), rows_ref[...], preferred_element_type=jnp.float32
    )
    out_ref[...] = made.reshape(experts, slots, columns).astype(out_ref.dtype)


def first_selection(ids, rows_in):
    rows, columns = rows_in.shape
    return pl.pallas_call(
        select_kernel,
        out_shape=[
            jax.ShapeDtypeStruct((EXPERTS, rows), jnp.float32),
            jax.ShapeDtypeStruct((EXPERTS, FIRST, columns), jnp.bfloat16),
        ],
        compiler_params=pltpu.CompilerParams(vmem_limit_bytes=MOST),
        cost_estimate=cost(EXPERTS * FIRST, rows, columns),
        name="first_selection",
    )(ids.T, rows_in)


def their_kernel(where, rows_ref, weight_ref, out_ref):
    out_ref[...] = jnp.dot(
        rows_ref[...], weight_ref[...], preferred_element_type=jnp.float32
    ).astype(out_ref.dtype)


def their_half(where, rows_in, weight):
    half, depth = rows_in.shape[0] // 2, rows_in.shape[1]
    columns = weight.shape[1]
    tile = min(256, half)
    steps = half // tile
    return pl.pallas_call(
        their_kernel,
        out_shape=jax.ShapeDtypeStruct((half, columns), jnp.bfloat16),
        grid_spec=pltpu.PrefetchScalarGridSpec(
            num_scalar_prefetch=1,
            grid=(steps,),
            in_specs=[
                pl.BlockSpec((tile, depth), lambda i, where: ((1 - where[0]) * steps + i, 0)),
                pl.BlockSpec((depth, columns), lambda i, where: (0, 0)),
            ],
            out_specs=pl.BlockSpec((tile, columns), lambda i, where: (i, 0)),
        ),
        compiler_params=pltpu.CompilerParams(vmem_limit_bytes=VMEM),
        cost_estimate=cost(half, depth, columns),
        name="their_half",
    )(where, rows_in, weight)


def own_kernel(where, rows_ref, weight_ref, arrived_ref, own_ref, *rest):
    piece_refs, total = rest[:-1], rest[-1]
    tile = rows_ref.shape[0]
    share = own_ref.shape[0]
    size = total.shape[0] // share
    step = pl.program_id(0)
    here = pl.ds(pl.multiple_of(step * tile, tile), tile)
    total[here, :] = jnp.dot(
        rows_ref[...], weight_ref[...], preferred_element_type=jnp.float32
    ) + arrived_ref[...].astype(jnp.float32)

    @pl.when(step == pl.num_programs(0) - 1)
    def _():
        if size == 1:
            own_ref[...] = total[...]
            piece_refs[0][...] = total[...].astype(jnp.bfloat16)
        else:
            for ahead in range(size):
                place = lax.rem(where[1] + ahead, size)
                piece = total[pl.ds(pl.multiple_of(place * share, share), share), :]
                if ahead == 0:
                    own_ref[...] = piece
                else:
                    piece_refs[ahead - 1][...] = piece.astype(jnp.bfloat16)


def own_half(where, rows_in, weight, arrived, size):
    half, depth = rows_in.shape[0] // 2, rows_in.shape[1]
    columns = weight.shape[1]
    tile = min(256, half)
    steps = half // tile
    share = half // size
    return pl.pallas_call(
        own_kernel,
        out_shape=[jax.ShapeDtypeStruct((share, columns), jnp.float32)]
        + [jax.ShapeDtypeStruct((share, columns), jnp.bfloat16)] * max(1, size - 1),
        grid_spec=pltpu.PrefetchScalarGridSpec(
            num_scalar_prefetch=1,
            grid=(steps,),
            in_specs=[
                pl.BlockSpec((tile, depth), lambda i, where: (where[0] * steps + i, 0)),
                pl.BlockSpec((depth, columns), lambda i, where: (0, 0)),
                pl.BlockSpec((tile, columns), lambda i, where: (i, 0)),
            ],
            out_specs=[pl.BlockSpec((share, columns), lambda i, where: (0, 0))]
            * max(2, size),
            scratch_shapes=[pltpu.VMEM((half, columns), jnp.float32)],
        ),
        compiler_params=pltpu.CompilerParams(vmem_limit_bytes=VMEM),
        cost_estimate=cost(half, depth, columns),
        name="own_half",
    )(where, rows_in, weight, arrived)


def combine_kernel(weights_ref, rows_ref, out_ref):
    out_ref[...] = jnp.dot(weights_ref[...], rows_ref[...], preferred_element_type=jnp.float32)


def combined(weights, rows_in):
    rows, depth = weights.shape
    columns = rows_in.shape[1]
    return pl.pallas_call(
        combine_kernel,
        out_shape=jax.ShapeDtypeStruct((rows, columns), jnp.float32),
        compiler_params=pltpu.CompilerParams(vmem_limit_bytes=MOST),
        cost_estimate=cost(rows, depth, columns),
        name="combined",
    )(weights, rows_in)


def copy_kernel(from_ref, to_ref):
    to_ref[...] = from_ref[...]


def copied(value):
    rows, columns = value.shape
    tile = 128
    return pl.pallas_call(
        copy_kernel,
        out_shape=jax.ShapeDtypeStruct(value.shape, value.dtype),
        grid=(rows // tile,),
        in_specs=[pl.BlockSpec((tile, columns), lambda i: (i, 0))],
        out_specs=pl.BlockSpec((tile, columns), lambda i: (i, 0)),
        compiler_params=pltpu.CompilerParams(vmem_limit_bytes=VMEM),
        cost_estimate=pl.CostEstimate(
            flops=0, bytes_accessed=4 * rows * columns, transcendentals=0
        ),
        name="copied",
    )(value)


def down_kernel(where, mine_ref, theirs_ref, weight_ref, out_ref):
    @pl.when(pl.program_id(0) == 0)
    def _():
        out_ref[...] = jnp.dot(
            mine_ref[...], weight_ref[...], preferred_element_type=jnp.float32
        ).astype(out_ref.dtype)

    @pl.when(pl.program_id(0) == 1)
    def _():
        out_ref[...] = jnp.dot(
            theirs_ref[...], weight_ref[...], preferred_element_type=jnp.float32
        ).astype(out_ref.dtype)


def down_both(where, mine, theirs, weight):
    half, depth = mine.shape
    columns = weight.shape[2]
    return pl.pallas_call(
        down_kernel,
        out_shape=jax.ShapeDtypeStruct((2 * half, columns), jnp.bfloat16),
        grid_spec=pltpu.PrefetchScalarGridSpec(
            num_scalar_prefetch=1,
            grid=(2,),
            in_specs=[
                pl.BlockSpec((half, depth), lambda h, where: (0, 0)),
                pl.BlockSpec((half, depth), lambda h, where: (0, 0)),
                pl.BlockSpec((None, depth, columns), lambda h, where: (0, 0, 0)),
            ],
            out_specs=pl.BlockSpec(
                (half, columns), lambda h, where: (where[0] + h - 2 * where[0] * h, 0)
            ),
        ),
        compiler_params=pltpu.CompilerParams(vmem_limit_bytes=VMEM),
        cost_estimate=cost(2 * half, depth, columns),
        name="down_both",
    )(where, mine, theirs, weight)


def wide_kernel(where, rows_ref, weight_ref, other_ref, *out_refs):
    depth = weight_ref.shape[0]
    share = out_refs[0].shape[0]
    size = len(out_refs)
    for ahead, out_ref in enumerate(out_refs):
        place = lax.rem(where[1] + ahead, size)
        rows = rows_ref[pl.ds(pl.multiple_of(place * share, share), share), :]
        made = jnp.dot(
            rows[:, :depth], weight_ref[...], preferred_element_type=jnp.float32
        ) + jnp.dot(rows[:, depth:], other_ref[...], preferred_element_type=jnp.float32)
        out_ref[...] = made.astype(out_ref.dtype)


def wide_product(where, rows_in, weight, other, size):
    rows, width = rows_in.shape
    depth, columns = weight.shape
    share = rows // size
    return pl.pallas_call(
        wide_kernel,
        out_shape=[jax.ShapeDtypeStruct((share, columns), jnp.float32)]
        + [jax.ShapeDtypeStruct((share, columns), jnp.bfloat16)] * (size - 1),
        grid_spec=pltpu.PrefetchScalarGridSpec(
            num_scalar_prefetch=1,
            grid=(1,),
            in_specs=[
                pl.BlockSpec((rows, width), lambda i, where: (0, 0)),
                pl.BlockSpec((depth, columns), lambda i, where: (0, 0)),
                pl.BlockSpec((depth, columns), lambda i, where: (0, 0)),
            ],
            out_specs=[pl.BlockSpec((share, columns), lambda i, where: (0, 0))] * size,
        ),
        compiler_params=pltpu.CompilerParams(vmem_limit_bytes=VMEM),
        cost_estimate=cost(rows, width, columns),
        name="wide_product",
    )(where, rows_in, weight, other)


def down_half_kernel(where, rows_ref, weight_ref, *rest):
    out_ref = rest[-1]
    sources, _, slots, columns = out_ref.shape
    size = 4
    share = sources // size
    together = rows_ref.shape[0] // (share * slots)
    made = jnp.dot(rows_ref[...], weight_ref[...], preferred_element_type=jnp.float32)
    for k in range(together):
        back = pl.program_id(0) * together + k
        step = jnp.where(back < 2, back, 5 - back)
        place = lax.rem(where[1] + size - step, size)
        piece = made[k * share * slots : (k + 1) * share * slots]
        out_ref[pl.ds(place * share, share), 0] = piece.reshape(share, slots, columns).astype(
            out_ref.dtype
        )


def down_half(where, core, rows_in, weight, made, sources):
    rows, depth = rows_in.shape
    columns = weight.shape[2]
    slots = rows // sources
    tile = rows // 2
    in_specs = [
        pl.BlockSpec((tile, depth), lambda i, where: (i, 0)),
        pl.BlockSpec((None, depth, columns), lambda i, where: (0, 0, 0)),
    ]
    inputs = [rows_in, weight]
    aliases = {}
    if made is not None:
        in_specs.append(pl.BlockSpec(memory_space=pl.ANY))
        inputs.append(made)
        aliases = {3: 0}

    def half(i, where):
        return 0, where[0] + core - 2 * where[0] * core, 0, 0

    return pl.pallas_call(
        down_half_kernel,
        out_shape=jax.ShapeDtypeStruct((sources, 2, slots, columns), jnp.bfloat16),
        grid_spec=pltpu.PrefetchScalarGridSpec(
            num_scalar_prefetch=1,
            grid=(rows // tile,),
            in_specs=in_specs,
            out_specs=pl.BlockSpec((sources, 1, slots, columns), half),
        ),
        input_output_aliases=aliases,
        compiler_params=pltpu.CompilerParams(vmem_limit_bytes=VMEM),
        cost_estimate=cost(rows, depth, columns),
        name="down_half",
    )(where, *inputs)


def narrow_rows(where, rows_in, up, down):
    arrived = turned(their_half(where, rows_in, up), "role", 1)
    own, rounded = own_half(where, rows_in, up, arrived, 1)
    pieces = [turned(rounded, "tp", step) for step in (3, 1, 2)]
    for piece in pieces:
        own = own + piece.astype(jnp.float32)
    mine = jax.nn.silu(own).astype(jnp.bfloat16)
    return down_both(where, mine, turned(mine, "role", 1), down)


def wide_rows(where, rows_in, up, other_up, down, sources):
    size = lax.axis_size("tp")
    own, *pieces = wide_product(where, rows_in, up, other_up, size)
    for step in (3, 1, 2):
        own = own + turned(pieces[step - 1], "tp", step).astype(jnp.float32)
    mine = jax.nn.silu(own).astype(jnp.bfloat16)
    others = {step: turned(mine, "tp", step) for step in (3, 1, 2)}
    mine = jnp.concatenate([mine, others[1], others[3], others[2]], axis=0)
    theirs = turned(mine, "role", 1)
    made = down_half(where, 0, mine, down, None, sources)
    return down_half(where, 1, theirs, down, made, sources)


def shards(
    q_latent,
    key_value_cache,
    cache_lengths,
    hidden,
    expert_ids,
    route_logits,
    up_weight,
    down_weight,
):
    rows, width = hidden.shape
    owners = lax.axis_size("grp")
    experts = jnp.arange(EXPERTS, dtype=jnp.int32)
    where = jnp.stack([lax.axis_index("role"), lax.axis_index("tp")]).astype(jnp.int32)

    rank, first_out = first_selection(expert_ids, hidden)

    def exchanged(value):
        return lax.all_to_all(value, "grp", split_axis=0, concat_axis=0, tiled=True)

    def outgoing(first, count, source):
        slots = (first + jnp.arange(count, dtype=jnp.int32)).astype(jnp.float32)
        placed = rank[:, None, :] == slots[None, :, None]
        placed = placed.reshape(-1, rows).astype(jnp.bfloat16)
        made = jnp.dot(placed, source, preferred_element_type=jnp.float32).astype(jnp.bfloat16)
        return made.reshape(owners, count, source.shape[1])

    def weights(first, last):
        slots = jnp.arange(first, last, dtype=jnp.int32).astype(jnp.float32)
        taken = rank.T[:, :, None] == slots[None, None, :]
        return jnp.where(taken, weight_of[:, :, None], 0.0).reshape(rows, -1).astype(jnp.bfloat16)

    first_out, hidden = lax.optimization_barrier((first_out, hidden))
    first_in = exchanged(first_out)

    wide = jnp.concatenate([hidden, turned(hidden, "role", 1)], axis=1)
    passed_up = copied(up_weight[0])

    sigmoid_terms = jax.nn.sigmoid(route_logits)
    route_weights = 2.5 * sigmoid_terms / jnp.sum(sigmoid_terms, axis=-1, keepdims=True)
    named = expert_ids[:, None, :] == experts[None, :, None]
    weight_of = jnp.sum(jnp.where(named, route_weights[:, None, :], 0.0), axis=2)
    weights_of = [weights(0, FIRST), weights(FIRST, CAP)]

    half = (CAP - FIRST) // 2
    begin = FIRST + where[0] * half
    second_out, first_in, passed_up, *weights_of = lax.optimization_barrier(
        (outgoing(begin, half, wide), first_in, passed_up, *weights_of)
    )
    second_in = exchanged(second_out)
    other_up = turned(passed_up, "role", 1)
    first_out = narrow_rows(where, first_in.reshape(-1, width), up_weight[0], down_weight)
    second_in, first_out = lax.optimization_barrier((second_in, first_out))
    first_back = exchanged(first_out.reshape(owners, FIRST, width))
    second_out = wide_rows(where, second_in.reshape(-1, 2 * width), up_weight[0], other_up, down_weight, owners)
    second_out, first_back, q_latent = lax.optimization_barrier((second_out, first_back, q_latent))
    second_back = exchanged(second_out)

    packed = attention_part(q_latent, key_value_cache, cache_lengths)
    size = lax.axis_size("tp")
    heads = q_latent.shape[1] // size
    place = lax.axis_index("tp")
    pieces = [
        lax.dynamic_slice_in_dim(packed, (place + step) % size * heads, heads, 1)
        for step in range(size)
    ]
    pieces = [pieces[0]] + [turned(pieces[step], "tp", step) for step in (2, 1, 3)]
    attn_context = attention_join(pieces)
    first_back = first_back.reshape(-1, width)
    second_back = second_back.reshape(-1, width)
    result = combined(weights_of[0], first_back)
    result = result + jnp.dot(weights_of[1], second_back, preferred_element_type=jnp.float32)
    return (attn_context, result.astype(jnp.bfloat16))


def solution(mesh):
    return jax.shard_map(
        shards,
        mesh=mesh,
        in_specs=(
            P(("role", "grp"), None, None),
            P(("role", "grp"), "tp", None),
            P(("role", "grp")),
            P("grp", ("role", "tp")),
            P("grp", None),
            P("grp", None),
            P("grp", ("role", "tp"), None),
            P("grp", None, ("role", "tp")),
        ),
        out_specs=(P(("role", "grp"), "tp", None), P("grp", ("role", "tp"))),
        check_vma=False,
    )
```
